32 devices in a mesh: dp: 16 (over z, x, core), section: 2 (over y).
Axes of the slice: x: 2, y: 2, z: 4, core: 2. Of those that a mesh axis runs over, the one named last changes fastest.
Arguments:
- features: bfloat16 [32, 16, 5120], P('dp'), may hold values from -6 to 6
- target: bfloat16 [32, 16, 5120], P('dp'), may hold values from -6 to 6
- timesteps: int32 [32], P('dp'), may hold values from 0 to 999
- conv_one: bfloat16 [2, 2880, 320], P('section'), may hold values from -0.109375 to 0.109375
- conv_two: bfloat16 [2, 2880, 320], P('section'), may hold values from -0.109375 to 0.109375
- time_proj: float32 [2, 320, 320], P('section'), may hold values from -0.3125 to 0.3125
Outputs:
- grad_one: float32 [2, 2880, 320], P('section')
- grad_two: float32 [2, 2880, 320], P('section')
- grad_time: float32 [2, 320, 320], P('section')
The draws below stay inside these ranges and needn't reach their ends.
All inputs are finite; a program needn't handle non-finite values.
Results may differ from the reference program's by a relative error of at most 0.002.
Values sent between devices are 32-bit elements; how exact they have to be, the bound alone decides.
A program may use at most 128 MiB of HBM per device.

```python
import math
import jax
import jax.numpy as jnp
from jax import lax

CH = 320
TE = 320
GROUPS = 32
HEIGHT = 16
WIDTH = 16
BATCH = 32
KROWS = 2880
SECTIONS = 2
N_SECTION = 2


def place_ends(drawn, own_key, low, largest):
    place = [jax.random.randint(jax.random.fold_in(own_key, axis), (), 0, length) for axis, length in enumerate(drawn.shape)]
    widest = drawn.shape.index(max(drawn.shape))
    next_to = place[:widest] + [(place[widest] + 1) % drawn.shape[widest]] + place[widest + 1:]
    return drawn.at[tuple(place)].set(low).at[tuple(next_to)].set(largest)


def steps_of(rng, extent, split, least, high):
    level = 1.0
    for position, parts in split:
        heights = jax.random.uniform(jax.random.fold_in(jax.random.fold_in(rng, 6), position), (parts,), jnp.float32, least / len(split), high / len(split))
        level = level * jnp.repeat(jnp.exp(heights), extent[position] // parts).reshape((-1,) + (1,) * (len(extent) - 1 - position))
    return level


def normal_values(own_key, extent, scale, limit, shards=(), kind=jnp.bfloat16):
    factor_of = steps_of(own_key, extent, shards, -0.22, 0.18) if shards else 1.0
    drawn = jax.random.normal(own_key, extent, jnp.float32) * scale * factor_of
    return jnp.minimum(jnp.maximum(drawn, -limit), limit).astype(kind)


def setup_inputs(seed: int = 0) -> dict:
    streams_of = jax.random.split(jax.random.key(seed), 7)
    return {
        "features": normal_values(streams_of[0], (BATCH, HEIGHT, WIDTH * CH), 1.0, 6.0, ((0, 16),)),
        "target": normal_values(streams_of[1], (BATCH, HEIGHT, WIDTH * CH), 1.0, 6.0, ((0, 16),)),
        "timesteps": place_ends(jax.random.randint(streams_of[2], (BATCH,), 0, 1000), jax.random.fold_in(streams_of[2], 1), 0, 999).astype(jnp.int32),
        "conv_one": normal_values(streams_of[3], (SECTIONS, KROWS, CH), KROWS ** -0.5, 0.109375, ((0, 2),)),
        "conv_two": normal_values(streams_of[4], (SECTIONS, KROWS, CH), KROWS ** -0.5, 0.109375, ((0, 2),)),
        "time_proj": normal_values(streams_of[5], (SECTIONS, TE, CH), TE ** -0.5, 0.3125, ((0, 2),), jnp.float32),
    }


def embed_times(times):
    middle = TE // 2
    freqs = jnp.exp(-math.log(10000.0) * jnp.arange(middle, dtype=jnp.float32) / middle)
    angles = times.astype(jnp.float32)[:, None] * freqs[None, :]
    return jnp.concatenate([jnp.cos(angles), jnp.sin(angles)], axis=1)

def norm_silu(values):
    count, height, width, chans = values.shape
    grouped = values.reshape(count, height, width, GROUPS, chans // GROUPS)
    center = lax.optimization_barrier(jnp.mean(grouped, axis=(1, 2, 4), keepdims=True))
    spread = lax.optimization_barrier(jnp.mean(jnp.square(grouped - center), axis=(1, 2, 4), keepdims=True))
    normed = ((grouped - center) * lax.rsqrt(spread + 1e-05)).reshape(values.shape)
    return jax.nn.silu(normed)

def patches(acts):
    height, width = (acts.shape[1], acts.shape[2])
    padded = jnp.pad(acts, ((0, 0), (1, 1), (1, 1), (0, 0)))
    taps = [padded[:, row_shift:row_shift + height, col_shift:col_shift + width, :] for row_shift in range(3) for col_shift in range(3)]
    return jnp.concatenate(taps, axis=-1)

def conv_apply(acts, weights):
    cols = patches(acts)
    flat = cols.reshape(-1, cols.shape[-1])
    result = jnp.dot(flat, weights, preferred_element_type=jnp.float32)
    return result.reshape(acts.shape[:3] + (weights.shape[1],))

def conv_back(grads, weights):
    count, height, width, chans = grads.shape
    flat = grads.reshape(-1, chans)
    spread_back = jnp.dot(flat, weights.T, preferred_element_type=jnp.float32)
    in_chans = weights.shape[0] // 9
    spread_back = spread_back.reshape(count, height, width, 9, in_chans)
    padded = jnp.zeros((count, height + 2, width + 2, in_chans), jnp.float32)
    for index in range(9):
        row_shift, col_shift = (index // 3, index % 3)
        padded = padded.at[:, row_shift:row_shift + height, col_shift:col_shift + width, :].add(spread_back[:, :, :, index, :])
    return padded[:, 1:-1, 1:-1, :]

def weight_grad(acts, grads):
    cols = patches(acts)
    flat = cols.reshape(-1, cols.shape[-1])
    return lax.dot_general(flat, grads.reshape(-1, grads.shape[-1]), (((0,), (0,)), ((), ())), preferred_element_type=jnp.float32)

def section_forward(section_in, bias_rows, weight_one, weight_two):
    acts_one = norm_silu(section_in).astype(jnp.bfloat16)
    conv_mid = conv_apply(acts_one, weight_one) + bias_rows[:, None, None, :]
    acts_two = norm_silu(conv_mid).astype(jnp.bfloat16)
    return section_in + conv_apply(acts_two, weight_two)

def section_backward(section_in, bias_rows, weight_one, weight_two, grad_out):
    acts_one = norm_silu(section_in).astype(jnp.bfloat16)
    conv_mid = conv_apply(acts_one, weight_one) + bias_rows[:, None, None, :]
    acts_two = norm_silu(conv_mid).astype(jnp.bfloat16)
    grad_low = grad_out.astype(jnp.bfloat16)
    delta_two = weight_grad(acts_two, grad_low)
    grad_acts_two = conv_back(grad_low, weight_two)
    grad_mid = jax.vjp(norm_silu, conv_mid)[1](grad_acts_two)[0]
    grad_bias = lax.optimization_barrier(jnp.sum(grad_mid, axis=(1, 2)))
    grad_mid_low = grad_mid.astype(jnp.bfloat16)
    delta_one = weight_grad(acts_one, grad_mid_low)
    grad_acts_one = conv_back(grad_mid_low, weight_one)
    grad_in = grad_out + jax.vjp(norm_silu, section_in)[1](grad_acts_one)[0]
    return (grad_in, delta_one, delta_two, grad_bias)

def reference(features, target, timesteps, conv_one, conv_two, time_proj):
    batch = features.shape[0]
    middle = N_SECTION // 2
    embedded = embed_times(timesteps)
    current = features.reshape(batch, HEIGHT, WIDTH, CH).astype(jnp.float32)
    inputs_kept = []
    outputs_kept = []
    biases_kept = []
    for section in range(N_SECTION):
        bias_rows = jnp.dot(embedded, time_proj[section], precision=lax.Precision.HIGHEST)
        section_in = current
        if section >= middle:
            section_in = section_in + outputs_kept[N_SECTION - 1 - section]
        result = section_forward(section_in, bias_rows, conv_one[section], conv_two[section])
        inputs_kept.append(section_in)
        outputs_kept.append(result)
        biases_kept.append(bias_rows)
        current = result
    scale = 1.0 / math.sqrt(HEIGHT * WIDTH)
    target_img = target.reshape(batch, HEIGHT, WIDTH, CH)
    grad_next = (current - target_img.astype(jnp.float32)) * scale
    skip_grads = {}
    ones = [None] * N_SECTION
    twos = [None] * N_SECTION
    times_out = [None] * N_SECTION
    for section in range(N_SECTION - 1, -1, -1):
        grad_out = grad_next
        if section < middle:
            grad_out = grad_out + skip_grads[section]
        grad_in, delta_one, delta_two, grad_bias = section_backward(inputs_kept[section], biases_kept[section], conv_one[section], conv_two[section], grad_out)
        ones[section] = delta_one
        twos[section] = delta_two
        times_out[section] = jnp.dot(embedded.T, grad_bias, precision=lax.Precision.HIGHEST)
        grad_next = grad_in
        if section >= middle:
            skip_grads[N_SECTION - 1 - section] = grad_next
    return (jnp.stack(ones), jnp.stack(twos), jnp.stack(times_out))
```

```python
import math

import jax
import jax.numpy as jnp
from jax import lax
from jax.experimental import pallas as pl
from jax.experimental.pallas import tpu as pltpu
from jax.sharding import PartitionSpec as P

CH = 320
TE = 320
GROUPS = 32
HEIGHT = 16
WIDTH = 16
MICRO = 2


def from_partner(value, axis, apart):
    mask = 2**apart
    pairs = [(source, source ^ mask) for source in range(lax.axis_size(axis))]
    return lax.ppermute(value, axis, pairs)


def passed_along(block, axis, distance):
    devices = range(lax.axis_size(axis))
    route = [(i - distance, i) for i in devices if i - distance in devices]
    return lax.ppermute(block, axis, route)


def embed_times(times):
    middle = TE // 2
    freqs = jnp.exp(-math.log(10000.0) * jnp.arange(middle, dtype=jnp.float32) / middle)
    angles = times.astype(jnp.float32)[:, None] * freqs[None, :]
    return jnp.concatenate([jnp.cos(angles), jnp.sin(angles)], axis=1)


def norm_silu(values):
    count, height, width, chans = values.shape
    grouped = values.reshape(count, height, width, GROUPS, chans // GROUPS)
    center = jnp.mean(grouped, axis=(1, 2, 4), keepdims=True)
    spread = jnp.mean(jnp.square(grouped - center), axis=(1, 2, 4), keepdims=True)
    normed = ((grouped - center) * lax.rsqrt(spread + 1e-05)).reshape(values.shape)
    return jax.nn.silu(normed)


def patches(acts):
    height, width = (acts.shape[1], acts.shape[2])
    padded = jnp.pad(acts, ((0, 0), (1, 1), (1, 1), (0, 0)))
    taps = [
        padded[:, row_shift : row_shift + height, col_shift : col_shift + width, :]
        for row_shift in range(3)
        for col_shift in range(3)
    ]
    return jnp.concatenate(taps, axis=-1)


def conv_apply(acts, weights):
    cols = patches(acts)
    flat = cols.reshape(-1, cols.shape[-1])
    result = jnp.dot(flat, weights, preferred_element_type=jnp.float32)
    return result.reshape(acts.shape[:3] + (weights.shape[1],))


def conv_back(grads, weights):
    count, height, width, chans = grads.shape
    flat = grads.reshape(-1, chans)
    spread_back = jnp.dot(flat, weights.T, preferred_element_type=jnp.float32)
    in_chans = weights.shape[0] // 9
    spread_back = spread_back.reshape(count, height, width, 9, in_chans)
    padded = jnp.zeros((count, height + 2, width + 2, in_chans), jnp.float32)
    for index in range(9):
        row_shift, col_shift = (index // 3, index % 3)
        padded = padded.at[:, row_shift : row_shift + height, col_shift : col_shift + width, :].add(
            spread_back[:, :, :, index, :]
        )
    return padded[:, 1:-1, 1:-1, :]


def weight_grad(acts, grads):
    cols = patches(acts)
    flat = cols.reshape(-1, cols.shape[-1])
    return lax.dot_general(
        flat,
        grads.reshape(-1, grads.shape[-1]),
        (((0,), (0,)), ((), ())),
        preferred_element_type=jnp.float32,
    )


def section_forward(section_in, bias_rows, weight_one, weight_two):
    acts_one = norm_silu(section_in).astype(jnp.bfloat16)
    conv_mid = conv_apply(acts_one, weight_one) + bias_rows[:, None, None, :]
    acts_two = norm_silu(conv_mid).astype(jnp.bfloat16)
    return section_in + conv_apply(acts_two, weight_two)


def section_backward(section_in, bias_rows, weight_one, weight_two, grad_out):
    acts_one = norm_silu(section_in).astype(jnp.bfloat16)
    conv_mid = conv_apply(acts_one, weight_one) + bias_rows[:, None, None, :]
    acts_two = norm_silu(conv_mid).astype(jnp.bfloat16)
    grad_low = grad_out.astype(jnp.bfloat16)
    delta_two = weight_grad(acts_two, grad_low)
    grad_acts_two = conv_back(grad_low, weight_two)
    grad_mid = jax.vjp(norm_silu, conv_mid)[1](grad_acts_two)[0]
    grad_bias = jnp.sum(grad_mid, axis=(1, 2))
    grad_mid_low = grad_mid.astype(jnp.bfloat16)
    delta_one = weight_grad(acts_one, grad_mid_low)
    grad_acts_one = conv_back(grad_mid_low, weight_one)
    grad_in = grad_out + jax.vjp(norm_silu, section_in)[1](grad_acts_one)[0]
    return (grad_in, delta_one, delta_two, grad_bias)


def pick_slot(buffer, slot):
    return lax.dynamic_index_in_dim(buffer, slot, 0, keepdims=False)


def put_slot(buffer, slot, value, enabled):
    fresh = jnp.where(enabled, value, pick_slot(buffer, slot))
    return lax.dynamic_update_index_in_dim(buffer, fresh, slot, 0)


def local(features, target, timesteps, conv_one, conv_two, time_proj):
    sections = lax.axis_size("section")
    section_pos = lax.axis_index("section")
    middle = sections // 2
    partner = sections - 1 - section_pos
    is_decoder = section_pos >= middle
    is_encoder = section_pos < middle
    is_first = section_pos == 0
    is_last = section_pos == sections - 1
    images = features.shape[0] // MICRO
    row_len = WIDTH * CH
    weight_one = conv_one[0]
    weight_two = conv_two[0]
    embedded = embed_times(timesteps)
    bias_all = jnp.dot(embedded, time_proj[0], precision=lax.Precision.HIGHEST)
    feats_micro = features.reshape(MICRO, images, HEIGHT, row_len)
    target_micro = target.reshape(MICRO, images, HEIGHT, row_len)
    bias_micro = bias_all.reshape(MICRO, images, CH)
    embed_micro = embedded.reshape(MICRO, images, TE)
    tick_count = MICRO + sections - 1
    bit_count = sections.bit_length() - 1
    bit_list = list(range(bit_count))
    image_shape = (images, HEIGHT, WIDTH, CH)
    flat_shape = (images, HEIGHT, row_len)
    stack_shape = (middle,) + flat_shape
    scale = 1.0 / math.sqrt(HEIGHT * WIDTH)

    def route_forward(sent):
        moved = sent
        for bit in bit_list:
            moved = from_partner(moved, "section", bit)
        return moved

    def route_backward(sent):
        moved = sent
        for bit in bit_list:
            moved = from_partner(moved, "section", bit)
        return moved

    def forward_tick(carry, tick):
        incoming, skip_buffer, skip_stack, saved_inputs, last_outputs = carry
        micro_now = tick - section_pos
        active = (micro_now >= 0) & (micro_now < MICRO)
        slot = jnp.clip(micro_now, 0, MICRO - 1)
        given = jnp.where(is_first, pick_slot(feats_micro, slot).astype(jnp.float32), incoming)
        skip_now = pick_slot(skip_buffer, slot)
        skip_part = jnp.where(is_decoder, skip_now, 0.0)
        section_in = (given + skip_part).reshape(image_shape)
        bias_rows = pick_slot(bias_micro, slot)
        result = lax.cond(
            active,
            lambda: section_forward(section_in, bias_rows, weight_one, weight_two),
            lambda: jnp.zeros(image_shape, jnp.float32),
        )
        result = result.reshape(flat_shape)
        saved_inputs = put_slot(saved_inputs, slot, section_in, active)
        last_outputs = put_slot(last_outputs, slot, result, active & is_last)
        incoming = passed_along(result, "section", 1)
        arrived = route_forward(result)
        skip_micro = tick - partner
        usable = is_decoder & (skip_micro >= 0) & (skip_micro < MICRO)
        skip_slot = jnp.clip(skip_micro, 0, MICRO - 1)
        skip_buffer = put_slot(skip_buffer, skip_slot, arrived, usable)
        return ((incoming, skip_buffer, skip_stack, saved_inputs, last_outputs), None)

    start_fwd = (
        jnp.zeros(flat_shape, jnp.float32),
        jnp.zeros((MICRO,) + flat_shape, jnp.float32),
        jnp.zeros(stack_shape, jnp.float32),
        jnp.zeros((MICRO,) + image_shape, jnp.float32),
        jnp.zeros((MICRO,) + flat_shape, jnp.float32),
    )
    fwd_done, unused_out = lax.scan(forward_tick, start_fwd, jnp.arange(tick_count))
    saved_inputs, last_outputs = (fwd_done[3], fwd_done[4])

    def backward_tick(carry, tick):
        incoming, skip_grads, grad_stack, total_one, total_two, total_time = carry
        micro_now = tick - (sections - 1 - section_pos)
        active = (micro_now >= 0) & (micro_now < MICRO)
        slot = jnp.clip(micro_now, 0, MICRO - 1)
        loss_grad = (
            pick_slot(last_outputs, slot) - pick_slot(target_micro, slot).astype(jnp.float32)
        ) * scale
        given = jnp.where(is_last, loss_grad, incoming)
        skip_now = pick_slot(skip_grads, slot)
        given = given + jnp.where(is_encoder, skip_now, 0.0)
        grad_out = given.reshape(image_shape)
        section_in = pick_slot(saved_inputs, slot)
        bias_rows = pick_slot(bias_micro, slot)

        def run_section():
            return section_backward(section_in, bias_rows, weight_one, weight_two, grad_out)

        def quiet_section():
            return (
                jnp.zeros(image_shape, jnp.float32),
                jnp.zeros(weight_one.shape, jnp.float32),
                jnp.zeros(weight_two.shape, jnp.float32),
                jnp.zeros((images, CH), jnp.float32),
            )

        grad_in, delta_one, delta_two, grad_bias = lax.cond(active, run_section, quiet_section)
        delta_time = jnp.dot(
            pick_slot(embed_micro, slot).T, grad_bias, precision=lax.Precision.HIGHEST
        )
        grad_flat = grad_in.reshape(flat_shape)
        incoming = passed_along(grad_flat, "section", -1)
        arrived = route_backward(grad_flat)
        skip_micro = tick - section_pos
        usable = is_encoder & (skip_micro >= 0) & (skip_micro < MICRO)
        skip_slot = jnp.clip(skip_micro, 0, MICRO - 1)
        skip_grads = put_slot(skip_grads, skip_slot, arrived, usable)
        return (
            (
                incoming,
                skip_grads,
                grad_stack,
                total_one + delta_one,
                total_two + delta_two,
                total_time + delta_time,
            ),
            None,
        )

    start_bwd = (
        jnp.zeros(flat_shape, jnp.float32),
        jnp.zeros((MICRO,) + flat_shape, jnp.float32),
        jnp.zeros(stack_shape, jnp.float32),
        jnp.zeros(weight_one.shape, jnp.float32),
        jnp.zeros(weight_two.shape, jnp.float32),
        jnp.zeros((TE, CH), jnp.float32),
    )
    finished, unused_back = lax.scan(backward_tick, start_bwd, jnp.arange(tick_count))
    total_one, total_two, total_time = (finished[3], finished[4], finished[5])
    sum_one, sum_two, sum_time = lax.psum((total_one, total_two, total_time), "dp")
    return (sum_one[None], sum_two[None], sum_time[None])


PIX = HEIGHT * WIDTH
KR = 3 * CH
MESH_IDS = pl.DeviceIdType.MESH
VMEM_BYTES = 56 * 1024 * 1024


def group_mean(cols, same_group):
    wide = jnp.broadcast_to(cols, (8, CH))
    total = jnp.dot(
        wide, same_group, precision=lax.Precision.HIGHEST, preferred_element_type=jnp.float32
    )
    return total[0:1, :] * (1.0 / (PIX * (CH // GROUPS)))


def col_sum(values):
    return jnp.sum(values, axis=0, keepdims=True)


def norm_parts(values, same_group):
    centered = values - group_mean(col_sum(values), same_group)
    inv = lax.rsqrt(group_mean(col_sum(centered * centered), same_group) + 1e-05)
    normed = centered * inv
    gate = 1.0 / (1.0 + jnp.exp(-normed))
    return normed, gate, inv


def norm_back(parts, cotangent, same_group):
    normed, gate, inv = parts
    dn = cotangent * (gate * (1.0 + normed * (1.0 - gate)))
    mean_dn = group_mean(col_sum(dn), same_group)
    mean_dnn = group_mean(col_sum(dn * normed), same_group)
    return inv * (dn - mean_dn - normed * mean_dnn)


def side_taps(values):
    column = lax.broadcasted_iota(jnp.int32, (PIX, CH), 0) % WIDTH
    before = jnp.where(column == 0, 0.0, pltpu.roll(values, 1, 0))
    after = jnp.where(column == WIDTH - 1, 0.0, pltpu.roll(values, PIX - 1, 0))
    return before, values, after


def stack_taps(parts):
    return jnp.concatenate(parts, axis=1).astype(jnp.bfloat16)


def add_rows(low, mid, high):
    edge = jnp.zeros((WIDTH, CH), jnp.float32)
    down = jnp.concatenate([edge, low[: PIX - WIDTH]], axis=0)
    up = jnp.concatenate([high[WIDTH:], edge], axis=0)
    return down + mid + up


def images_of(rows):
    return [rows[i * PIX : (i + 1) * PIX] for i in range(rows.shape[0] // PIX)]


def conv_rows(taps, w_ref):
    parts = [
        jnp.dot(taps, w_ref[r * KR : (r + 1) * KR, :], preferred_element_type=jnp.float32)
        for r in range(3)
    ]
    split = [images_of(part) for part in parts]
    return [add_rows(*trio) for trio in zip(*split)]


def conv_rows_back(low_rows, w_ref):
    before, same, after = [
        jnp.concatenate(part, axis=0).astype(jnp.bfloat16)
        for part in zip(*[side_taps(rows) for rows in low_rows])
    ]
    sums = []
    for r in range(3):
        total = None
        for c, side in enumerate((after, same, before)):
            tap = (3 * r + c) * CH
            part = lax.dot_general(
                side, w_ref[tap : tap + CH, :], (((1,), (1,)), ((), ())),
                preferred_element_type=jnp.float32,
            )
            total = part if total is None else total + part
        sums.append(images_of(total))
    return [add_rows(up, mid, down) for down, mid, up in zip(*sums)]


def weight_rows(taps, low_rows, buf_ref, lane):
    edge = jnp.zeros((WIDTH, CH), jnp.float32)
    flipped = taps.T
    for r in range(3):
        moved = []
        for rows in low_rows:
            if r == 0:
                moved.append(jnp.concatenate([rows[WIDTH:], edge], axis=0))
            elif r == 1:
                moved.append(rows)
            else:
                moved.append(jnp.concatenate([edge, rows[: PIX - WIDTH]], axis=0))
        side = jnp.concatenate(moved, axis=0).astype(jnp.bfloat16)
        buf_ref[r * KR : (r + 1) * KR, lane : lane + CH] = jnp.dot(
            flipped, side, preferred_element_type=jnp.float32
        )


def rounded(values):
    return values.astype(jnp.bfloat16).astype(jnp.float32)


def taps_of(parts):
    return jnp.concatenate([stack_taps(side_taps(n * g)) for n, g, _ in parts], axis=0)


def forward_rows(inputs, bias_ref, w1_ref, w2_ref, same_group):
    parts_a = [norm_parts(v, same_group) for v in inputs]
    taps_a = taps_of(parts_a)
    mids = conv_rows(taps_a, w1_ref)
    mids = [mid + bias_ref[i : i + 1, :] for i, mid in enumerate(mids)]
    parts_b = [norm_parts(v, same_group) for v in mids]
    taps_b = taps_of(parts_b)
    outs = conv_rows(taps_b, w2_ref)
    return mids, [v + o for v, o in zip(inputs, outs)], parts_a, taps_a, parts_b, taps_b


def backward_rows(grads, kept, emb_ref, w1_ref, w2_ref, same_group, buf_ref):
    parts_a, taps_a, parts_b, taps_b = kept
    low = [rounded(g) for g in grads]
    weight_rows(taps_b, low, buf_ref, CH)
    back = conv_rows_back(low, w2_ref)
    grad_mid = [norm_back(p, b, same_group) for p, b in zip(parts_b, back)]
    d_time = None
    for i, gm in enumerate(grad_mid):
        part = emb_ref[:, i : i + 1] * col_sum(gm)
        d_time = part if d_time is None else d_time + part
    buf_ref[9 * CH : 9 * CH + TE // 2, 0:CH] = d_time[: TE // 2]
    buf_ref[9 * CH : 9 * CH + TE // 2, CH : 2 * CH] = d_time[TE // 2 :]
    pad = buf_ref.shape[0] - 9 * CH - TE // 2
    buf_ref[9 * CH + TE // 2 :, :] = jnp.zeros((pad, 2 * CH), jnp.float32)
    low = [rounded(g) for g in grad_mid]
    weight_rows(taps_a, low, buf_ref, 0)
    back = conv_rows_back(low, w1_ref)
    return [g + norm_back(p, b, same_group) for g, p, b in zip(grads, parts_a, back)]


def put_images(ref, images):
    for i, image in enumerate(images):
        ref[i * PIX : (i + 1) * PIX, :] = image


def first_kernel(x_ref, bias_ref, w1_ref, w2_ref, same_ref, mid_ref, y_ref):
    inputs = images_of(x_ref[...].astype(jnp.float32))
    mids, outs, *_ = forward_rows(inputs, bias_ref, w1_ref, w2_ref, same_ref[...])
    put_images(mid_ref, mids)
    put_images(y_ref, outs)


def last_kernel(y_ref, target_ref, bias_ref, emb_ref, w1_ref, w2_ref, same_ref, gu_ref, buf_ref):
    same = same_ref[...]
    inputs = [y + y for y in images_of(y_ref[...])]
    _, outs, *kept = forward_rows(inputs, bias_ref, w1_ref, w2_ref, same)
    wanted = images_of(target_ref[...].astype(jnp.float32))
    scale = 1.0 / math.sqrt(PIX)
    grads = [(o - w) * scale for o, w in zip(outs, wanted)]
    put_images(gu_ref, backward_rows(grads, kept, emb_ref, w1_ref, w2_ref, same, buf_ref))


def return_kernel(x_ref, mid_ref, gu_ref, emb_ref, w1_ref, w2_ref, same_ref, buf_ref):
    same = same_ref[...]
    parts_a = [norm_parts(v, same) for v in images_of(x_ref[...].astype(jnp.float32))]
    parts_b = [norm_parts(v, same) for v in images_of(mid_ref[...])]
    kept = (parts_a, taps_of(parts_a), parts_b, taps_of(parts_b))
    grads = [g + g for g in images_of(gu_ref[...])]
    backward_rows(grads, kept, emb_ref, w1_ref, w2_ref, same, buf_ref)


def in_vmem(kernel, name, outs):
    return pl.pallas_call(
        kernel,
        name=name,
        out_shape=outs,
        compiler_params=pltpu.CompilerParams(vmem_limit_bytes=VMEM_BYTES),
    )


def buffer_rows(replicas):
    step = 8 * 2 * replicas
    return -(-(9 * CH + TE // 2) // step) * step


def local_two(features, target, timesteps, conv_one, conv_two, time_proj):
    section_pos = lax.axis_index("section")
    images = features.shape[0]
    rows = images * PIX
    x = features.reshape(rows, CH)
    wanted = target.reshape(rows, CH)
    w1, w2 = conv_one[0], conv_two[0]
    embedded = embed_times(timesteps)
    bias = jnp.dot(embedded, time_proj[0], precision=lax.Precision.HIGHEST)
    emb = embedded.T
    group = jnp.arange(CH) // (CH // GROUPS)
    same = (group[:, None] == group[None, :]).astype(jnp.float32)
    flat = jax.ShapeDtypeStruct((rows, CH), jnp.float32)
    packed_rows = buffer_rows(lax.axis_size("dp"))
    packed = jax.ShapeDtypeStruct((packed_rows, 2 * CH), jnp.float32)

    def blank(shape):
        return jnp.zeros(shape.shape, shape.dtype)

    mid, y = lax.cond(
        section_pos == 0,
        lambda: tuple(in_vmem(first_kernel, "first", [flat, flat])(x, bias, w1, w2, same)),
        lambda: (blank(flat), blank(flat)),
    )
    y = lax.ppermute(y, "section", [(0, 1)])
    gu, buf = lax.cond(
        section_pos == 1,
        lambda: tuple(
            in_vmem(last_kernel, "last", [flat, packed])(y, wanted, bias, emb, w1, w2, same)
        ),
        lambda: (blank(flat), blank(packed)),
    )
    gu = lax.ppermute(gu, "section", [(1, 0)])
    buf = lax.cond(
        section_pos == 0,
        lambda: in_vmem(return_kernel, "back", packed)(x, mid, gu, emb, w1, w2, same),
        lambda: buf,
    )
    buf = sum_over_dp(buf)
    d_time = jnp.concatenate(
        [buf[9 * CH : 9 * CH + TE // 2, :CH], buf[9 * CH : 9 * CH + TE // 2, CH:]], axis=0
    )
    return (buf[None, : 9 * CH, :CH], buf[None, : 9 * CH, CH:], d_time[None])


def sum_over_dp(buf):
    return lax.psum(buf, "dp")


def solution(mesh):
    placed = (
        P("dp", None, None),
        P("dp", None, None),
        P("dp"),
        P("section", None, None),
        P("section", None, None),
        P("section", None, None),
    )
    body = local_two if mesh.shape["section"] == 2 else local
    return jax.shard_map(
        body,
        mesh=mesh,
        in_specs=placed,
        out_specs=(P("section", None, None), P("section", None, None), P("section", None, None)),
        check_vma=False,
    )
```

```python
import math

import jax
import jax.numpy as jnp
from jax import lax
from jax.experimental import pallas as pl
from jax.experimental.pallas import tpu as pltpu
from jax.sharding import PartitionSpec as P

CH = 320
TE = 320
GROUPS = 32
HEIGHT = 16
WIDTH = 16
MICRO = 2


def from_partner(value, axis, apart):
    mask = 2**apart
    pairs = [(source, source ^ mask) for source in range(lax.axis_size(axis))]
    return lax.ppermute(value, axis, pairs)


def passed_along(block, axis, distance):
    devices = range(lax.axis_size(axis))
    route = [(i - distance, i) for i in devices if i - distance in devices]
    return lax.ppermute(block, axis, route)


def embed_times(times):
    middle = TE // 2
    freqs = jnp.exp(-math.log(10000.0) * jnp.arange(middle, dtype=jnp.float32) / middle)
    angles = times.astype(jnp.float32)[:, None] * freqs[None, :]
    return jnp.concatenate([jnp.cos(angles), jnp.sin(angles)], axis=1)


def norm_silu(values):
    count, height, width, chans = values.shape
    grouped = values.reshape(count, height, width, GROUPS, chans // GROUPS)
    center = jnp.mean(grouped, axis=(1, 2, 4), keepdims=True)
    spread = jnp.mean(jnp.square(grouped - center), axis=(1, 2, 4), keepdims=True)
    normed = ((grouped - center) * lax.rsqrt(spread + 1e-05)).reshape(values.shape)
    return jax.nn.silu(normed)


def patches(acts):
    height, width = (acts.shape[1], acts.shape[2])
    padded = jnp.pad(acts, ((0, 0), (1, 1), (1, 1), (0, 0)))
    taps = [
        padded[:, row_shift : row_shift + height, col_shift : col_shift + width, :]
        for row_shift in range(3)
        for col_shift in range(3)
    ]
    return jnp.concatenate(taps, axis=-1)


def conv_apply(acts, weights):
    cols = patches(acts)
    flat = cols.reshape(-1, cols.shape[-1])
    result = jnp.dot(flat, weights, preferred_element_type=jnp.float32)
    return result.reshape(acts.shape[:3] + (weights.shape[1],))


def conv_back(grads, weights):
    count, height, width, chans = grads.shape
    flat = grads.reshape(-1, chans)
    spread_back = jnp.dot(flat, weights.T, preferred_element_type=jnp.float32)
    in_chans = weights.shape[0] // 9
    spread_back = spread_back.reshape(count, height, width, 9, in_chans)
    padded = jnp.zeros((count, height + 2, width + 2, in_chans), jnp.float32)
    for index in range(9):
        row_shift, col_shift = (index // 3, index % 3)
        padded = padded.at[:, row_shift : row_shift + height, col_shift : col_shift + width, :].add(
            spread_back[:, :, :, index, :]
        )
    return padded[:, 1:-1, 1:-1, :]


def weight_grad(acts, grads):
    cols = patches(acts)
    flat = cols.reshape(-1, cols.shape[-1])
    return lax.dot_general(
        flat,
        grads.reshape(-1, grads.shape[-1]),
        (((0,), (0,)), ((), ())),
        preferred_element_type=jnp.float32,
    )


def section_forward(section_in, bias_rows, weight_one, weight_two):
    acts_one = norm_silu(section_in).astype(jnp.bfloat16)
    conv_mid = conv_apply(acts_one, weight_one) + bias_rows[:, None, None, :]
    acts_two = norm_silu(conv_mid).astype(jnp.bfloat16)
    return section_in + conv_apply(acts_two, weight_two)


def section_backward(section_in, bias_rows, weight_one, weight_two, grad_out):
    acts_one = norm_silu(section_in).astype(jnp.bfloat16)
    conv_mid = conv_apply(acts_one, weight_one) + bias_rows[:, None, None, :]
    acts_two = norm_silu(conv_mid).astype(jnp.bfloat16)
    grad_low = grad_out.astype(jnp.bfloat16)
    delta_two = weight_grad(acts_two, grad_low)
    grad_acts_two = conv_back(grad_low, weight_two)
    grad_mid = jax.vjp(norm_silu, conv_mid)[1](grad_acts_two)[0]
    grad_bias = jnp.sum(grad_mid, axis=(1, 2))
    grad_mid_low = grad_mid.astype(jnp.bfloat16)
    delta_one = weight_grad(acts_one, grad_mid_low)
    grad_acts_one = conv_back(grad_mid_low, weight_one)
    grad_in = grad_out + jax.vjp(norm_silu, section_in)[1](grad_acts_one)[0]
    return (grad_in, delta_one, delta_two, grad_bias)


def pick_slot(buffer, slot):
    return lax.dynamic_index_in_dim(buffer, slot, 0, keepdims=False)


def put_slot(buffer, slot, value, enabled):
    fresh = jnp.where(enabled, value, pick_slot(buffer, slot))
    return lax.dynamic_update_index_in_dim(buffer, fresh, slot, 0)


def local(features, target, timesteps, conv_one, conv_two, time_proj):
    sections = lax.axis_size("section")
    section_pos = lax.axis_index("section")
    middle = sections // 2
    partner = sections - 1 - section_pos
    is_decoder = section_pos >= middle
    is_encoder = section_pos < middle
    is_first = section_pos == 0
    is_last = section_pos == sections - 1
    images = features.shape[0] // MICRO
    row_len = WIDTH * CH
    weight_one = conv_one[0]
    weight_two = conv_two[0]
    embedded = embed_times(timesteps)
    bias_all = jnp.dot(embedded, time_proj[0], precision=lax.Precision.HIGHEST)
    feats_micro = features.reshape(MICRO, images, HEIGHT, row_len)
    target_micro = target.reshape(MICRO, images, HEIGHT, row_len)
    bias_micro = bias_all.reshape(MICRO, images, CH)
    embed_micro = embedded.reshape(MICRO, images, TE)
    tick_count = MICRO + sections - 1
    bit_count = sections.bit_length() - 1
    bit_list = list(range(bit_count))
    image_shape = (images, HEIGHT, WIDTH, CH)
    flat_shape = (images, HEIGHT, row_len)
    stack_shape = (middle,) + flat_shape
    scale = 1.0 / math.sqrt(HEIGHT * WIDTH)

    def route_forward(sent):
        moved = sent
        for bit in bit_list:
            moved = from_partner(moved, "section", bit)
        return moved

    def route_backward(sent):
        moved = sent
        for bit in bit_list:
            moved = from_partner(moved, "section", bit)
        return moved

    def forward_tick(carry, tick):
        incoming, skip_buffer, skip_stack, saved_inputs, last_outputs = carry
        micro_now = tick - section_pos
        active = (micro_now >= 0) & (micro_now < MICRO)
        slot = jnp.clip(micro_now, 0, MICRO - 1)
        given = jnp.where(is_first, pick_slot(feats_micro, slot).astype(jnp.float32), incoming)
        skip_now = pick_slot(skip_buffer, slot)
        skip_part = jnp.where(is_decoder, skip_now, 0.0)
        section_in = (given + skip_part).reshape(image_shape)
        bias_rows = pick_slot(bias_micro, slot)
        result = lax.cond(
            active,
            lambda: section_forward(section_in, bias_rows, weight_one, weight_two),
            lambda: jnp.zeros(image_shape, jnp.float32),
        )
        result = result.reshape(flat_shape)
        saved_inputs = put_slot(saved_inputs, slot, section_in, active)
        last_outputs = put_slot(last_outputs, slot, result, active & is_last)
        incoming = passed_along(result, "section", 1)
        arrived = route_forward(result)
        skip_micro = tick - partner
        usable = is_decoder & (skip_micro >= 0) & (skip_micro < MICRO)
        skip_slot = jnp.clip(skip_micro, 0, MICRO - 1)
        skip_buffer = put_slot(skip_buffer, skip_slot, arrived, usable)
        return ((incoming, skip_buffer, skip_stack, saved_inputs, last_outputs), None)

    start_fwd = (
        jnp.zeros(flat_shape, jnp.float32),
        jnp.zeros((MICRO,) + flat_shape, jnp.float32),
        jnp.zeros(stack_shape, jnp.float32),
        jnp.zeros((MICRO,) + image_shape, jnp.float32),
        jnp.zeros((MICRO,) + flat_shape, jnp.float32),
    )
    fwd_done, unused_out = lax.scan(forward_tick, start_fwd, jnp.arange(tick_count))
    saved_inputs, last_outputs = (fwd_done[3], fwd_done[4])

    def backward_tick(carry, tick):
        incoming, skip_grads, grad_stack, total_one, total_two, total_time = carry
        micro_now = tick - (sections - 1 - section_pos)
        active = (micro_now >= 0) & (micro_now < MICRO)
        slot = jnp.clip(micro_now, 0, MICRO - 1)
        loss_grad = (
            pick_slot(last_outputs, slot) - pick_slot(target_micro, slot).astype(jnp.float32)
        ) * scale
        given = jnp.where(is_last, loss_grad, incoming)
        skip_now = pick_slot(skip_grads, slot)
        given = given + jnp.where(is_encoder, skip_now, 0.0)
        grad_out = given.reshape(image_shape)
        section_in = pick_slot(saved_inputs, slot)
        bias_rows = pick_slot(bias_micro, slot)

        def run_section():
            return section_backward(section_in, bias_rows, weight_one, weight_two, grad_out)

        def quiet_section():
            return (
                jnp.zeros(image_shape, jnp.float32),
                jnp.zeros(weight_one.shape, jnp.float32),
                jnp.zeros(weight_two.shape, jnp.float32),
                jnp.zeros((images, CH), jnp.float32),
            )

        grad_in, delta_one, delta_two, grad_bias = lax.cond(active, run_section, quiet_section)
        delta_time = jnp.dot(
            pick_slot(embed_micro, slot).T, grad_bias, precision=lax.Precision.HIGHEST
        )
        grad_flat = grad_in.reshape(flat_shape)
        incoming = passed_along(grad_flat, "section", -1)
        arrived = route_backward(grad_flat)
        skip_micro = tick - section_pos
        usable = is_encoder & (skip_micro >= 0) & (skip_micro < MICRO)
        skip_slot = jnp.clip(skip_micro, 0, MICRO - 1)
        skip_grads = put_slot(skip_grads, skip_slot, arrived, usable)
        return (
            (
                incoming,
                skip_grads,
                grad_stack,
                total_one + delta_one,
                total_two + delta_two,
                total_time + delta_time,
            ),
            None,
        )

    start_bwd = (
        jnp.zeros(flat_shape, jnp.float32),
        jnp.zeros((MICRO,) + flat_shape, jnp.float32),
        jnp.zeros(stack_shape, jnp.float32),
        jnp.zeros(weight_one.shape, jnp.float32),
        jnp.zeros(weight_two.shape, jnp.float32),
        jnp.zeros((TE, CH), jnp.float32),
    )
    finished, unused_back = lax.scan(backward_tick, start_bwd, jnp.arange(tick_count))
    total_one, total_two, total_time = (finished[3], finished[4], finished[5])
    sum_one, sum_two, sum_time = lax.psum((total_one, total_two, total_time), "dp")
    return (sum_one[None], sum_two[None], sum_time[None])


PIX = HEIGHT * WIDTH
KR = 3 * CH
MESH_IDS = pl.DeviceIdType.MESH
VMEM_BYTES = 56 * 1024 * 1024


def group_mean(cols, same_group):
    wide = jnp.broadcast_to(cols, (8, CH))
    total = jnp.dot(
        wide, same_group, precision=lax.Precision.HIGHEST, preferred_element_type=jnp.float32
    )
    return total[0:1, :] * (1.0 / (PIX * (CH // GROUPS)))


def col_sum(values):
    return jnp.sum(values, axis=0, keepdims=True)


def norm_parts(values, same_group):
    centered = values - group_mean(col_sum(values), same_group)
    inv = lax.rsqrt(group_mean(col_sum(centered * centered), same_group) + 1e-05)
    normed = centered * inv
    gate = 1.0 / (1.0 + jnp.exp(-normed))
    return normed, gate, inv


def norm_back(parts, cotangent, same_group):
    normed, gate, inv = parts
    dn = cotangent * (gate * (1.0 + normed * (1.0 - gate)))
    mean_dn = group_mean(col_sum(dn), same_group)
    mean_dnn = group_mean(col_sum(dn * normed), same_group)
    return inv * (dn - mean_dn - normed * mean_dnn)


def side_taps(values):
    column = lax.broadcasted_iota(jnp.int32, (PIX, CH), 0) % WIDTH
    before = jnp.where(column == 0, 0.0, pltpu.roll(values, 1, 0))
    after = jnp.where(column == WIDTH - 1, 0.0, pltpu.roll(values, PIX - 1, 0))
    return before, values, after


def stack_taps(parts):
    return jnp.concatenate(parts, axis=1).astype(jnp.bfloat16)


def add_rows(low, mid, high):
    edge = jnp.zeros((WIDTH, CH), jnp.float32)
    down = jnp.concatenate([edge, low[: PIX - WIDTH]], axis=0)
    up = jnp.concatenate([high[WIDTH:], edge], axis=0)
    return down + mid + up


def images_of(rows):
    return [rows[i * PIX : (i + 1) * PIX] for i in range(rows.shape[0] // PIX)]


def conv_rows(taps, w_ref):
    parts = [
        jnp.dot(taps, w_ref[r * KR : (r + 1) * KR, :], preferred_element_type=jnp.float32)
        for r in range(3)
    ]
    split = [images_of(part) for part in parts]
    return [add_rows(*trio) for trio in zip(*split)]


def conv_rows_back(low_rows, w_ref):
    before, same, after = [
        jnp.concatenate(part, axis=0).astype(jnp.bfloat16)
        for part in zip(*[side_taps(rows) for rows in low_rows])
    ]
    sums = []
    for r in range(3):
        total = None
        for c, side in enumerate((after, same, before)):
            tap = (3 * r + c) * CH
            part = lax.dot_general(
                side, w_ref[tap : tap + CH, :], (((1,), (1,)), ((), ())),
                preferred_element_type=jnp.float32,
            )
            total = part if total is None else total + part
        sums.append(images_of(total))
    return [add_rows(up, mid, down) for down, mid, up in zip(*sums)]


def weight_rows(taps, low_rows, buf_ref, lane):
    edge = jnp.zeros((WIDTH, CH), jnp.float32)
    flipped = taps.T
    for r in range(3):
        moved = []
        for rows in low_rows:
            if r == 0:
                moved.append(jnp.concatenate([rows[WIDTH:], edge], axis=0))
            elif r == 1:
                moved.append(rows)
            else:
                moved.append(jnp.concatenate([edge, rows[: PIX - WIDTH]], axis=0))
        side = jnp.concatenate(moved, axis=0).astype(jnp.bfloat16)
        buf_ref[r * KR : (r + 1) * KR, lane : lane + CH] = jnp.dot(
            flipped, side, preferred_element_type=jnp.float32
        )


def rounded(values):
    return values.astype(jnp.bfloat16).astype(jnp.float32)


def taps_of(parts):
    return jnp.concatenate([stack_taps(side_taps(n * g)) for n, g, _ in parts], axis=0)


def forward_rows(inputs, bias_ref, w1_ref, w2_ref, same_group):
    parts_a = [norm_parts(v, same_group) for v in inputs]
    taps_a = taps_of(parts_a)
    mids = conv_rows(taps_a, w1_ref)
    mids = [mid + bias_ref[i : i + 1, :] for i, mid in enumerate(mids)]
    parts_b = [norm_parts(v, same_group) for v in mids]
    taps_b = taps_of(parts_b)
    outs = conv_rows(taps_b, w2_ref)
    return mids, [v + o for v, o in zip(inputs, outs)], parts_a, taps_a, parts_b, taps_b


def backward_rows(grads, kept, emb_ref, w1_ref, w2_ref, same_group, buf_ref):
    parts_a, taps_a, parts_b, taps_b = kept
    low = [rounded(g) for g in grads]
    weight_rows(taps_b, low, buf_ref, CH)
    back = conv_rows_back(low, w2_ref)
    grad_mid = [norm_back(p, b, same_group) for p, b in zip(parts_b, back)]
    d_time = None
    for i, gm in enumerate(grad_mid):
        part = emb_ref[:, i : i + 1] * col_sum(gm)
        d_time = part if d_time is None else d_time + part
    buf_ref[9 * CH : 9 * CH + TE // 2, 0:CH] = d_time[: TE // 2]
    buf_ref[9 * CH : 9 * CH + TE // 2, CH : 2 * CH] = d_time[TE // 2 :]
    pad = buf_ref.shape[0] - 9 * CH - TE // 2
    buf_ref[9 * CH + TE // 2 :, :] = jnp.zeros((pad, 2 * CH), jnp.float32)
    low = [rounded(g) for g in grad_mid]
    weight_rows(taps_a, low, buf_ref, 0)
    back = conv_rows_back(low, w1_ref)
    return [g + norm_back(p, b, same_group) for g, p, b in zip(grads, parts_a, back)]


def put_images(ref, images):
    for i, image in enumerate(images):
        ref[i * PIX : (i + 1) * PIX, :] = image


def first_kernel(x_ref, bias_ref, w1_ref, w2_ref, same_ref, mid_ref, y_ref):
    inputs = images_of(x_ref[...].astype(jnp.float32))
    mids, outs, *_ = forward_rows(inputs, bias_ref, w1_ref, w2_ref, same_ref[...])
    put_images(mid_ref, mids)
    put_images(y_ref, outs)


def last_kernel(y_ref, target_ref, bias_ref, emb_ref, w1_ref, w2_ref, same_ref, gu_ref, buf_ref):
    same = same_ref[...]
    inputs = [y + y for y in images_of(y_ref[...])]
    _, outs, *kept = forward_rows(inputs, bias_ref, w1_ref, w2_ref, same)
    wanted = images_of(target_ref[...].astype(jnp.float32))
    scale = 1.0 / math.sqrt(PIX)
    grads = [(o - w) * scale for o, w in zip(outs, wanted)]
    put_images(gu_ref, backward_rows(grads, kept, emb_ref, w1_ref, w2_ref, same, buf_ref))


def return_kernel(x_ref, mid_ref, gu_ref, emb_ref, w1_ref, w2_ref, same_ref, buf_ref):
    same = same_ref[...]
    parts_a = [norm_parts(v, same) for v in images_of(x_ref[...].astype(jnp.float32))]
    parts_b = [norm_parts(v, same) for v in images_of(mid_ref[...])]
    kept = (parts_a, taps_of(parts_a), parts_b, taps_of(parts_b))
    grads = [g + g for g in images_of(gu_ref[...])]
    backward_rows(grads, kept, emb_ref, w1_ref, w2_ref, same, buf_ref)


def in_vmem(kernel, name, outs):
    return pl.pallas_call(
        kernel,
        name=name,
        out_shape=outs,
        compiler_params=pltpu.CompilerParams(vmem_limit_bytes=VMEM_BYTES),
    )


def buffer_rows(replicas):
    step = 8 * replicas * SUBS
    return -(-(9 * CH + TE // 2) // step) * step


def local_two(features, target, timesteps, conv_one, conv_two, time_proj):
    section_pos = lax.axis_index("section")
    images = features.shape[0]
    rows = images * PIX
    x = features.reshape(rows, CH)
    wanted = target.reshape(rows, CH)
    w1, w2 = conv_one[0], conv_two[0]
    embedded = embed_times(timesteps)
    bias = jnp.dot(embedded, time_proj[0], precision=lax.Precision.HIGHEST)
    emb = embedded.T
    group = jnp.arange(CH) // (CH // GROUPS)
    same = (group[:, None] == group[None, :]).astype(jnp.float32)
    flat = jax.ShapeDtypeStruct((rows, CH), jnp.float32)
    packed_rows = buffer_rows(lax.axis_size("dp"))
    packed = jax.ShapeDtypeStruct((packed_rows, 2 * CH), jnp.float32)

    def blank(shape):
        return jnp.zeros(shape.shape, shape.dtype)

    mid, y = lax.cond(
        section_pos == 0,
        lambda: tuple(in_vmem(first_kernel, "first", [flat, flat])(x, bias, w1, w2, same)),
        lambda: (blank(flat), blank(flat)),
    )
    y = lax.ppermute(y, "section", [(0, 1)])
    gu, buf = lax.cond(
        section_pos == 1,
        lambda: tuple(
            in_vmem(last_kernel, "last", [flat, packed])(y, wanted, bias, emb, w1, w2, same)
        ),
        lambda: (blank(flat), blank(packed)),
    )
    gu = lax.ppermute(gu, "section", [(1, 0)])
    buf = lax.cond(
        section_pos == 0,
        lambda: in_vmem(return_kernel, "back", packed)(x, mid, gu, emb, w1, w2, same),
        lambda: buf,
    )
    buf = sum_over_dp(buf)
    d_time = jnp.concatenate(
        [buf[9 * CH : 9 * CH + TE // 2, :CH], buf[9 * CH : 9 * CH + TE // 2, CH:]], axis=0
    )
    return (buf[None, : 9 * CH, :CH], buf[None, : 9 * CH, CH:], d_time[None])


CORES = 2
CHIPS = 8
SUBS = 2


def ring_places():
    dp = lax.axis_index("dp")
    core = dp % CORES
    chip = dp // CORES
    x, z = chip % 2, chip // 2
    place = z + x * (CHIPS - 1 - 2 * z)
    way = 1 - 2 * core

    def device(at):
        side = at // (CHIPS // 2)
        depth = at + side * (CHIPS - 1 - 2 * at)
        return {"dp": (depth * 2 + side) * CORES + core}

    after = device((place + way + CHIPS) % CHIPS)
    before = device((place - way + CHIPS) % CHIPS)
    sibling = {"dp": chip * CORES + 1 - core}
    return core, place, way, after, before, sibling


def ring_meet(after, before, sibling):
    barrier = pltpu.get_barrier_semaphore()
    for other in (after, before, sibling):
        pl.semaphore_signal(barrier, inc=1, device_id=other, device_id_type=MESH_IDS)
    pl.semaphore_wait(barrier, 3)


def ring_kernel(in_ref, out_ref, pair_ref, slot_ref, work_ref, pair_sems, step_sems, turn_sems, give_sems):
    core, place, way, after, before, sibling = ring_places()
    ring_meet(after, before, sibling)

    def remote(src, dst, sems, index, target):
        return pltpu.make_async_remote_copy(
            src_ref=src,
            dst_ref=dst,
            send_sem=sems.at[(0,) + index],
            recv_sem=sems.at[(1,) + index],
            device_id=target,
            device_id_type=MESH_IDS,
        )

    def block_at(step):
        return (place - way * step + 2 * CHIPS) % CHIPS

    def sibling_block_at(step):
        return (place + way * step + 2 * CHIPS) % CHIPS

    pending = []
    pairs = {}
    for step in range(CHIPS):
        for sub in range(SUBS):
            theirs = sibling_block_at(step)
            copy = remote(
                in_ref.at[1 - core, theirs, sub], pair_ref.at[step, sub], pair_sems, (step, sub), sibling
            )
            copy.start()
            pairs[step, sub] = copy
            pending.append(copy)

    arrived = {}
    for step in range(CHIPS):
        for sub in range(SUBS):
            block = block_at(step)
            pairs[step, sub].wait_recv()
            total = in_ref[core, block, sub] + pair_ref[step, sub]
            if step:
                arrived[step - 1, sub].wait_recv()
                total = total + slot_ref[step - 1, sub]
            if step < CHIPS - 1:
                work_ref[step, sub] = total
                copy = remote(
                    work_ref.at[step, sub], slot_ref.at[step, sub], step_sems, (step, sub), after
                )
                copy.start()
                arrived[step, sub] = copy
                pending.append(copy)
            else:
                out_ref[core, block, sub] = total

    turned = {}
    gifts = []
    for step in range(CHIPS):
        for sub in range(SUBS):
            block = block_at(CHIPS - 1 + step)
            if step:
                turned[step - 1, sub].wait_recv()
            here = out_ref.at[core, block, sub]
            if step < CHIPS - 1:
                copy = remote(here, here, turn_sems, (step, sub), after)
                copy.start()
                turned[step, sub] = copy
                pending.append(copy)
            copy = remote(here, here, give_sems, (step, sub), sibling)
            copy.start()
            gifts.append(copy)
    for copy in gifts:
        copy.wait_recv()
    for copy in pending + gifts:
        copy.wait_send()


def ring_scratch(part, lanes):
    return [
        pltpu.VMEM((CHIPS, SUBS, part, lanes), jnp.float32),
        pltpu.VMEM((CHIPS - 1, SUBS, part, lanes), jnp.float32),
        pltpu.VMEM((CHIPS - 1, SUBS, part, lanes), jnp.float32),
        pltpu.SemaphoreType.DMA((2, CHIPS, SUBS)),
        pltpu.SemaphoreType.DMA((2, CHIPS - 1, SUBS)),
        pltpu.SemaphoreType.DMA((2, CHIPS - 1, SUBS)),
        pltpu.SemaphoreType.DMA((2, CHIPS, SUBS)),
    ]


def sum_over_dp(buf):
    if lax.axis_size("dp") != CORES * CHIPS:
        return lax.psum(buf, "dp")
    rows, lanes = buf.shape
    part = rows // (CORES * CHIPS * SUBS)
    parts = (CORES, CHIPS, SUBS, part, lanes)
    total = pl.pallas_call(
        ring_kernel,
        name="ring",
        out_shape=jax.ShapeDtypeStruct(parts, jnp.float32),
        scratch_shapes=ring_scratch(part, lanes),
        compiler_params=pltpu.CompilerParams(
            collective_id=0, has_side_effects=True, vmem_limit_bytes=VMEM_BYTES
        ),
    )(buf.reshape(parts))
    return total.reshape(rows, lanes)


def solution(mesh):
    placed = (
        P("dp", None, None),
        P("dp", None, None),
        P("dp"),
        P("section", None, None),
        P("section", None, None),
        P("section", None, None),
    )
    body = local_two if mesh.shape["section"] == 2 else local
    return jax.shard_map(
        body,
        mesh=mesh,
        in_specs=placed,
        out_specs=(P("section", None, None), P("section", None, None), P("section", None, None)),
        check_vma=False,
    )
```

```python
import math

import jax
import jax.numpy as jnp
from jax import lax
from jax.experimental import pallas as pl
from jax.experimental.pallas import tpu as pltpu
from jax.sharding import PartitionSpec as P

CH = 320
TE = 320
GROUPS = 32
HEIGHT = 16
WIDTH = 16
MICRO = 2


def from_partner(value, axis, apart):
    mask = 2**apart
    pairs = [(source, source ^ mask) for source in range(lax.axis_size(axis))]
    return lax.ppermute(value, axis, pairs)


def passed_along(block, axis, distance):
    devices = range(lax.axis_size(axis))
    route = [(i - distance, i) for i in devices if i - distance in devices]
    return lax.ppermute(block, axis, route)


def embed_times(times):
    middle = TE // 2
    freqs = jnp.exp(-math.log(10000.0) * jnp.arange(middle, dtype=jnp.float32) / middle)
    angles = times.astype(jnp.float32)[:, None] * freqs[None, :]
    return jnp.concatenate([jnp.cos(angles), jnp.sin(angles)], axis=1)


def norm_silu(values):
    count, height, width, chans = values.shape
    grouped = values.reshape(count, height, width, GROUPS, chans // GROUPS)
    center = jnp.mean(grouped, axis=(1, 2, 4), keepdims=True)
    spread = jnp.mean(jnp.square(grouped - center), axis=(1, 2, 4), keepdims=True)
    normed = ((grouped - center) * lax.rsqrt(spread + 1e-05)).reshape(values.shape)
    return jax.nn.silu(normed)


def patches(acts):
    height, width = (acts.shape[1], acts.shape[2])
    padded = jnp.pad(acts, ((0, 0), (1, 1), (1, 1), (0, 0)))
    taps = [
        padded[:, row_shift : row_shift + height, col_shift : col_shift + width, :]
        for row_shift in range(3)
        for col_shift in range(3)
    ]
    return jnp.concatenate(taps, axis=-1)


def conv_apply(acts, weights):
    cols = patches(acts)
    flat = cols.reshape(-1, cols.shape[-1])
    result = jnp.dot(flat, weights, preferred_element_type=jnp.float32)
    return result.reshape(acts.shape[:3] + (weights.shape[1],))


def conv_back(grads, weights):
    count, height, width, chans = grads.shape
    flat = grads.reshape(-1, chans)
    spread_back = jnp.dot(flat, weights.T, preferred_element_type=jnp.float32)
    in_chans = weights.shape[0] // 9
    spread_back = spread_back.reshape(count, height, width, 9, in_chans)
    padded = jnp.zeros((count, height + 2, width + 2, in_chans), jnp.float32)
    for index in range(9):
        row_shift, col_shift = (index // 3, index % 3)
        padded = padded.at[:, row_shift : row_shift + height, col_shift : col_shift + width, :].add(
            spread_back[:, :, :, index, :]
        )
    return padded[:, 1:-1, 1:-1, :]


def weight_grad(acts, grads):
    cols = patches(acts)
    flat = cols.reshape(-1, cols.shape[-1])
    return lax.dot_general(
        flat,
        grads.reshape(-1, grads.shape[-1]),
        (((0,), (0,)), ((), ())),
        preferred_element_type=jnp.float32,
    )


def section_forward(section_in, bias_rows, weight_one, weight_two):
    acts_one = norm_silu(section_in).astype(jnp.bfloat16)
    conv_mid = conv_apply(acts_one, weight_one) + bias_rows[:, None, None, :]
    acts_two = norm_silu(conv_mid).astype(jnp.bfloat16)
    return section_in + conv_apply(acts_two, weight_two)


def section_backward(section_in, bias_rows, weight_one, weight_two, grad_out):
    acts_one = norm_silu(section_in).astype(jnp.bfloat16)
    conv_mid = conv_apply(acts_one, weight_one) + bias_rows[:, None, None, :]
    acts_two = norm_silu(conv_mid).astype(jnp.bfloat16)
    grad_low = grad_out.astype(jnp.bfloat16)
    delta_two = weight_grad(acts_two, grad_low)
    grad_acts_two = conv_back(grad_low, weight_two)
    grad_mid = jax.vjp(norm_silu, conv_mid)[1](grad_acts_two)[0]
    grad_bias = jnp.sum(grad_mid, axis=(1, 2))
    grad_mid_low = grad_mid.astype(jnp.bfloat16)
    delta_one = weight_grad(acts_one, grad_mid_low)
    grad_acts_one = conv_back(grad_mid_low, weight_one)
    grad_in = grad_out + jax.vjp(norm_silu, section_in)[1](grad_acts_one)[0]
    return (grad_in, delta_one, delta_two, grad_bias)


def pick_slot(buffer, slot):
    return lax.dynamic_index_in_dim(buffer, slot, 0, keepdims=False)


def put_slot(buffer, slot, value, enabled):
    fresh = jnp.where(enabled, value, pick_slot(buffer, slot))
    return lax.dynamic_update_index_in_dim(buffer, fresh, slot, 0)


def local(features, target, timesteps, conv_one, conv_two, time_proj):
    sections = lax.axis_size("section")
    section_pos = lax.axis_index("section")
    middle = sections // 2
    partner = sections - 1 - section_pos
    is_decoder = section_pos >= middle
    is_encoder = section_pos < middle
    is_first = section_pos == 0
    is_last = section_pos == sections - 1
    images = features.shape[0] // MICRO
    row_len = WIDTH * CH
    weight_one = conv_one[0]
    weight_two = conv_two[0]
    embedded = embed_times(timesteps)
    bias_all = jnp.dot(embedded, time_proj[0], precision=lax.Precision.HIGHEST)
    feats_micro = features.reshape(MICRO, images, HEIGHT, row_len)
    target_micro = target.reshape(MICRO, images, HEIGHT, row_len)
    bias_micro = bias_all.reshape(MICRO, images, CH)
    embed_micro = embedded.reshape(MICRO, images, TE)
    tick_count = MICRO + sections - 1
    bit_count = sections.bit_length() - 1
    bit_list = list(range(bit_count))
    image_shape = (images, HEIGHT, WIDTH, CH)
    flat_shape = (images, HEIGHT, row_len)
    stack_shape = (middle,) + flat_shape
    scale = 1.0 / math.sqrt(HEIGHT * WIDTH)

    def route_forward(sent):
        moved = sent
        for bit in bit_list:
            moved = from_partner(moved, "section", bit)
        return moved

    def route_backward(sent):
        moved = sent
        for bit in bit_list:
            moved = from_partner(moved, "section", bit)
        return moved

    def forward_tick(carry, tick):
        incoming, skip_buffer, skip_stack, saved_inputs, last_outputs = carry
        micro_now = tick - section_pos
        active = (micro_now >= 0) & (micro_now < MICRO)
        slot = jnp.clip(micro_now, 0, MICRO - 1)
        given = jnp.where(is_first, pick_slot(feats_micro, slot).astype(jnp.float32), incoming)
        skip_now = pick_slot(skip_buffer, slot)
        skip_part = jnp.where(is_decoder, skip_now, 0.0)
        section_in = (given + skip_part).reshape(image_shape)
        bias_rows = pick_slot(bias_micro, slot)
        result = lax.cond(
            active,
            lambda: section_forward(section_in, bias_rows, weight_one, weight_two),
            lambda: jnp.zeros(image_shape, jnp.float32),
        )
        result = result.reshape(flat_shape)
        saved_inputs = put_slot(saved_inputs, slot, section_in, active)
        last_outputs = put_slot(last_outputs, slot, result, active & is_last)
        incoming = passed_along(result, "section", 1)
        arrived = route_forward(result)
        skip_micro = tick - partner
        usable = is_decoder & (skip_micro >= 0) & (skip_micro < MICRO)
        skip_slot = jnp.clip(skip_micro, 0, MICRO - 1)
        skip_buffer = put_slot(skip_buffer, skip_slot, arrived, usable)
        return ((incoming, skip_buffer, skip_stack, saved_inputs, last_outputs), None)

    start_fwd = (
        jnp.zeros(flat_shape, jnp.float32),
        jnp.zeros((MICRO,) + flat_shape, jnp.float32),
        jnp.zeros(stack_shape, jnp.float32),
        jnp.zeros((MICRO,) + image_shape, jnp.float32),
        jnp.zeros((MICRO,) + flat_shape, jnp.float32),
    )
    fwd_done, unused_out = lax.scan(forward_tick, start_fwd, jnp.arange(tick_count))
    saved_inputs, last_outputs = (fwd_done[3], fwd_done[4])

    def backward_tick(carry, tick):
        incoming, skip_grads, grad_stack, total_one, total_two, total_time = carry
        micro_now = tick - (sections - 1 - section_pos)
        active = (micro_now >= 0) & (micro_now < MICRO)
        slot = jnp.clip(micro_now, 0, MICRO - 1)
        loss_grad = (
            pick_slot(last_outputs, slot) - pick_slot(target_micro, slot).astype(jnp.float32)
        ) * scale
        given = jnp.where(is_last, loss_grad, incoming)
        skip_now = pick_slot(skip_grads, slot)
        given = given + jnp.where(is_encoder, skip_now, 0.0)
        grad_out = given.reshape(image_shape)
        section_in = pick_slot(saved_inputs, slot)
        bias_rows = pick_slot(bias_micro, slot)

        def run_section():
            return section_backward(section_in, bias_rows, weight_one, weight_two, grad_out)

        def quiet_section():
            return (
                jnp.zeros(image_shape, jnp.float32),
                jnp.zeros(weight_one.shape, jnp.float32),
                jnp.zeros(weight_two.shape, jnp.float32),
                jnp.zeros((images, CH), jnp.float32),
            )

        grad_in, delta_one, delta_two, grad_bias = lax.cond(active, run_section, quiet_section)
        delta_time = jnp.dot(
            pick_slot(embed_micro, slot).T, grad_bias, precision=lax.Precision.HIGHEST
        )
        grad_flat = grad_in.reshape(flat_shape)
        incoming = passed_along(grad_flat, "section", -1)
        arrived = route_backward(grad_flat)
        skip_micro = tick - section_pos
        usable = is_encoder & (skip_micro >= 0) & (skip_micro < MICRO)
        skip_slot = jnp.clip(skip_micro, 0, MICRO - 1)
        skip_grads = put_slot(skip_grads, skip_slot, arrived, usable)
        return (
            (
                incoming,
                skip_grads,
                grad_stack,
                total_one + delta_one,
                total_two + delta_two,
                total_time + delta_time,
            ),
            None,
        )

    start_bwd = (
        jnp.zeros(flat_shape, jnp.float32),
        jnp.zeros((MICRO,) + flat_shape, jnp.float32),
        jnp.zeros(stack_shape, jnp.float32),
        jnp.zeros(weight_one.shape, jnp.float32),
        jnp.zeros(weight_two.shape, jnp.float32),
        jnp.zeros((TE, CH), jnp.float32),
    )
    finished, unused_back = lax.scan(backward_tick, start_bwd, jnp.arange(tick_count))
    total_one, total_two, total_time = (finished[3], finished[4], finished[5])
    sum_one, sum_two, sum_time = lax.psum((total_one, total_two, total_time), "dp")
    return (sum_one[None], sum_two[None], sum_time[None])


PIX = HEIGHT * WIDTH
KR = 3 * CH
MESH_IDS = pl.DeviceIdType.MESH
VMEM_BYTES = 56 * 1024 * 1024


def group_mean(cols, same_group):
    wide = jnp.broadcast_to(cols, (8, CH))
    total = jnp.dot(
        wide, same_group, precision=lax.Precision.HIGHEST, preferred_element_type=jnp.float32
    )
    return total[0:1, :] * (1.0 / (PIX * (CH // GROUPS)))


def col_sum(values):
    return jnp.sum(values, axis=0, keepdims=True)


def norm_parts(values, same_group):
    centered = values - group_mean(col_sum(values), same_group)
    inv = lax.rsqrt(group_mean(col_sum(centered * centered), same_group) + 1e-05)
    normed = centered * inv
    gate = 1.0 / (1.0 + jnp.exp(-normed))
    return normed, gate, inv


def norm_back(parts, cotangent, same_group):
    normed, gate, inv = parts
    dn = cotangent * (gate * (1.0 + normed * (1.0 - gate)))
    mean_dn = group_mean(col_sum(dn), same_group)
    mean_dnn = group_mean(col_sum(dn * normed), same_group)
    return inv * (dn - mean_dn - normed * mean_dnn)


def side_taps(values):
    column = lax.broadcasted_iota(jnp.int32, (PIX, CH), 0) % WIDTH
    before = jnp.where(column == 0, 0.0, pltpu.roll(values, 1, 0))
    after = jnp.where(column == WIDTH - 1, 0.0, pltpu.roll(values, PIX - 1, 0))
    return before, values, after


def add_rows(low, mid, high):
    edge = jnp.zeros((WIDTH, CH), jnp.float32)
    down = jnp.concatenate([edge, low[: PIX - WIDTH]], axis=0)
    up = jnp.concatenate([high[WIDTH:], edge], axis=0)
    return down + mid + up


def patch_rows(values):
    taps = jnp.concatenate(side_taps(values), axis=1).astype(jnp.bfloat16)
    edge = jnp.zeros((WIDTH, KR), jnp.bfloat16)
    above = jnp.concatenate([edge, taps[: PIX - WIDTH]], axis=0)
    below = jnp.concatenate([taps[WIDTH:], edge], axis=0)
    return jnp.concatenate([above, taps, below], axis=1)


def conv_rows_back(low, wt_ref):
    spread = jnp.dot(low, wt_ref[...], preferred_element_type=jnp.float32)
    cols = []
    for c in range(3):
        high, mid, down = [
            spread[:, (3 * r + c) * CH : (3 * r + c + 1) * CH] for r in range(3)
        ]
        cols.append(add_rows(down, mid, high))
    return side_taps(cols[2])[0] + cols[1] + side_taps(cols[0])[2]


def weight_rows(patches_low, low, buf_ref, first):
    buf_ref[first : first + CH, : 9 * CH] += jnp.dot(
        low.T, patches_low, preferred_element_type=jnp.float32
    )


def taps_of(parts):
    normed, gate, _ = parts
    return patch_rows(normed * gate)


def forward_rows(rows, bias, w1_ref, w2_ref, same_group):
    parts_a = norm_parts(rows, same_group)
    taps_a = taps_of(parts_a)
    mid = jnp.dot(taps_a, w1_ref[...], preferred_element_type=jnp.float32) + bias
    parts_b = norm_parts(mid, same_group)
    taps_b = taps_of(parts_b)
    out = rows + jnp.dot(taps_b, w2_ref[...], preferred_element_type=jnp.float32)
    return mid, out, parts_a, taps_a, parts_b, taps_b


def backward_rows(grad, kept, emb, wt1_ref, wt2_ref, same_group, buf_ref):
    parts_a, taps_a, parts_b, taps_b = kept
    low = grad.astype(jnp.bfloat16)
    back = conv_rows_back(low, wt2_ref)
    weight_rows(taps_b, low, buf_ref, CH)
    grad_mid = norm_back(parts_b, back, same_group)
    d_time = emb * col_sum(grad_mid)
    half = CH // 2
    buf_ref[0:TE, 9 * CH : 9 * CH + half] += d_time[:, :half]
    buf_ref[TE : 2 * TE, 9 * CH : 9 * CH + half] += d_time[:, half:]
    low = grad_mid.astype(jnp.bfloat16)
    weight_rows(taps_a, low, buf_ref, 0)
    back = conv_rows_back(low, wt1_ref)
    return grad + norm_back(parts_a, back, same_group)


CORES = 2
CHIPS = 8
BLOCK = 2 * CH // (CORES * CHIPS)
SPLITS = ((0, 24), (24, 16))
SUBS = len(SPLITS)
LANES = 3072


def ring_places():
    dp = lax.axis_index("dp")
    core = dp % CORES
    chip = dp // CORES
    x, z = chip % 2, chip // 2
    place = z + x * (CHIPS - 1 - 2 * z)
    way = 1 - 2 * core

    def device(at):
        side = at // (CHIPS // 2)
        depth = at + side * (CHIPS - 1 - 2 * at)
        return {"dp": (depth * 2 + side) * CORES + core}

    after = device((place + way + CHIPS) % CHIPS)
    before = device((place - way + CHIPS) % CHIPS)
    sibling = {"dp": chip * CORES + 1 - core}
    return core, place, way, after, before, sibling


def meet(others):
    barrier = pltpu.get_barrier_semaphore()
    for other in others:
        pl.semaphore_signal(barrier, inc=1, device_id=other, device_id_type=MESH_IDS)
    pl.semaphore_wait(barrier, len(others))


def ring_sum(places, in_ref, out_ref, pair_ref, slot_ref, work_ref, pair_sems, step_sems, turn_sems, give_sems):
    core, place, way, after, before, sibling = places

    def rows_of(half, block, sub):
        first, size = SPLITS[sub]
        start = (half * CHIPS + block) * BLOCK + first
        return pl.ds(pl.multiple_of(start, 8), size)

    def kept(ref, step, sub):
        first, size = SPLITS[sub]
        return ref.at[step, pl.ds(first, size)]

    def remote(src, dst, sems, index, target):
        return pltpu.make_async_remote_copy(
            src_ref=src,
            dst_ref=dst,
            send_sem=sems.at[(0,) + index],
            recv_sem=sems.at[(1,) + index],
            device_id=target,
            device_id_type=MESH_IDS,
        )

    def block_at(step):
        return (place - way * step + 2 * CHIPS) % CHIPS

    def sibling_block_at(step):
        return (place + way * step + 2 * CHIPS) % CHIPS

    pending = []
    pairs = {}
    for step in range(CHIPS):
        for sub in range(SUBS):
            theirs = sibling_block_at(step)
            copy = remote(
                in_ref.at[rows_of(1 - core, theirs, sub)], kept(pair_ref, step, sub), pair_sems, (step, sub), sibling
            )
            copy.start()
            pairs[step, sub] = copy
            pending.append(copy)

    arrived = {}
    for step in range(CHIPS):
        for sub in range(SUBS):
            block = block_at(step)
            pairs[step, sub].wait_recv()
            total = in_ref[rows_of(core, block, sub), :] + kept(pair_ref, step, sub)[...]
            if step:
                arrived[step - 1, sub].wait_recv()
                total = total + kept(slot_ref, step - 1, sub)[...]
            if step < CHIPS - 1:
                kept(work_ref, step, sub)[...] = total
                copy = remote(
                    kept(work_ref, step, sub), kept(slot_ref, step, sub), step_sems, (step, sub), after
                )
                copy.start()
                arrived[step, sub] = copy
                pending.append(copy)
            else:
                out_ref[rows_of(core, block, sub), :] = total

    turned = {}
    gifts = []
    for step in range(CHIPS):
        for sub in range(SUBS):
            block = block_at(CHIPS - 1 + step)
            if step:
                turned[step - 1, sub].wait_recv()
            here = out_ref.at[rows_of(core, block, sub)]
            if step < CHIPS - 1:
                copy = remote(here, here, turn_sems, (step, sub), after)
                copy.start()
                turned[step, sub] = copy
                pending.append(copy)
            copy = remote(here, here, give_sems, (step, sub), sibling)
            copy.start()
            gifts.append(copy)
    for copy in gifts:
        copy.wait_recv()
    for copy in pending + gifts:
        copy.wait_send()


def ring_scratch():
    return [
        pltpu.VMEM((CHIPS, BLOCK, LANES), jnp.float32),
        pltpu.VMEM((CHIPS - 1, BLOCK, LANES), jnp.float32),
        pltpu.VMEM((CHIPS - 1, BLOCK, LANES), jnp.float32),
        pltpu.SemaphoreType.DMA((2, CHIPS, SUBS)),
        pltpu.SemaphoreType.DMA((2, CHIPS - 1, SUBS)),
        pltpu.SemaphoreType.DMA((2, CHIPS - 1, SUBS)),
        pltpu.SemaphoreType.DMA((2, CHIPS, SUBS)),
    ]


def whole_kernel(
    x_ref, target_ref, bias_ref, emb_ref, wt1_ref, wt2_ref, same_ref,
    out_ref, w1_ref, w2_ref, mid_ref, send_ref, inbox_ref, buf_ref, send_sems, recv_sems, *ring_refs
):
    section = lax.axis_index("section")
    places = ring_places()
    partner = {"section": 1 - section}
    meet(places[3:] + (partner,))
    images = x_ref.shape[0]
    w1_ref[...] = wt1_ref[...].T
    w2_ref[...] = wt2_ref[...].T

    def sent(i):
        return pltpu.make_async_remote_copy(
            src_ref=send_ref.at[i],
            dst_ref=inbox_ref.at[i],
            send_sem=send_sems.at[i],
            recv_sem=recv_sems.at[i],
            device_id=partner,
            device_id_type=MESH_IDS,
        )

    @pl.when(section == 0)
    def _():
        @pl.loop(0, images)
        def _(i):
            rows = x_ref[i].astype(jnp.float32)
            mid, out, *_ = forward_rows(rows, bias_ref[i], w1_ref, w2_ref, same_ref[...])
            mid_ref[i] = mid
            send_ref[i] = out
            sent(i).start()

    buf_ref[...] = jnp.zeros(buf_ref.shape, jnp.float32)

    @pl.when(section == 0)
    def _():
        @pl.loop(0, images)
        def _(i):
            same = same_ref[...]
            parts_a = norm_parts(x_ref[i].astype(jnp.float32), same)
            parts_b = norm_parts(mid_ref[i], same)
            kept = (parts_a, taps_of(parts_a), parts_b, taps_of(parts_b))
            sent(i).wait_recv()
            grad = inbox_ref[i] + inbox_ref[i]
            backward_rows(grad, kept, emb_ref[i], wt1_ref, wt2_ref, same, buf_ref)

    @pl.when(section == 1)
    def _():
        @pl.loop(0, images)
        def _(i):
            same = same_ref[...]
            sent(i).wait_recv()
            rows = inbox_ref[i] + inbox_ref[i]
            _, out, *kept = forward_rows(rows, bias_ref[i], w1_ref, w2_ref, same)
            grad = (out - target_ref[i].astype(jnp.float32)) * (1.0 / math.sqrt(PIX))
            send_ref[i] = backward_rows(grad, kept, emb_ref[i], wt1_ref, wt2_ref, same, buf_ref)
            sent(i).start()

    for i in range(images):
        sent(i).wait_send()
    ring_sum(places, buf_ref, out_ref, *ring_refs)


def local_two(features, target, timesteps, conv_one, conv_two, time_proj):
    images = features.shape[0]
    x = features.reshape(images, PIX, CH)
    wanted = target.reshape(images, PIX, CH)
    embedded = embed_times(timesteps)
    bias = jnp.dot(embedded, time_proj[0], precision=lax.Precision.HIGHEST)
    group = jnp.arange(CH) // (CH // GROUPS)
    same = (group[:, None] == group[None, :]).astype(jnp.float32)
    stack = pltpu.VMEM((images, PIX, CH), jnp.float32)
    weight = pltpu.VMEM((9 * CH, CH), jnp.bfloat16)
    total = pl.pallas_call(
        whole_kernel,
        name="whole",
        out_shape=jax.ShapeDtypeStruct((2 * CH, LANES), jnp.float32),
        in_specs=[pl.BlockSpec(memory_space=pltpu.VMEM)] * 7,
        out_specs=pl.BlockSpec(memory_space=pltpu.VMEM),
        scratch_shapes=[
            weight,
            weight,
            stack,
            stack,
            stack,
            pltpu.VMEM((2 * CH, LANES), jnp.float32),
            pltpu.SemaphoreType.DMA((images,)),
            pltpu.SemaphoreType.DMA((images,)),
        ]
        + ring_scratch(),
        compiler_params=pltpu.CompilerParams(
            collective_id=0, has_side_effects=True, vmem_limit_bytes=VMEM_BYTES
        ),
    )(x, wanted, bias[:, None, :], embedded[:, :, None], conv_one[0].T, conv_two[0].T, same)
    one = total[:CH, : 9 * CH].T
    two = total[CH:, : 9 * CH].T
    tail = total[:, 9 * CH : 9 * CH + CH // 2]
    d_time = jnp.concatenate([tail[:TE], tail[TE:]], axis=1)
    return (one[None], two[None], d_time[None])


def solution(mesh):
    placed = (
        P("dp", None, None),
        P("dp", None, None),
        P("dp"),
        P("section", None, None),
        P("section", None, None),
        P("section", None, None),
    )
    two = mesh.shape["section"] == 2 and mesh.shape["dp"] == CORES * CHIPS
    body = local_two if two else local
    return jax.shard_map(
        body,
        mesh=mesh,
        in_specs=placed,
        out_specs=(P("section", None, None), P("section", None, None), P("section", None, None)),
        check_vma=False,
    )
```

```python
import math

import jax
import jax.numpy as jnp
from jax import lax
from jax.experimental import pallas as pl
from jax.experimental.pallas import tpu as pltpu
from jax.sharding import PartitionSpec as P

CH = 320
TE = 320
GROUPS = 32
HEIGHT = 16
WIDTH = 16
MICRO = 2


def from_partner(value, axis, apart):
    mask = 2**apart
    pairs = [(source, source ^ mask) for source in range(lax.axis_size(axis))]
    return lax.ppermute(value, axis, pairs)


def passed_along(block, axis, distance):
    devices = range(lax.axis_size(axis))
    route = [(i - distance, i) for i in devices if i - distance in devices]
    return lax.ppermute(block, axis, route)


def embed_times(times):
    middle = TE // 2
    freqs = jnp.exp(-math.log(10000.0) * jnp.arange(middle, dtype=jnp.float32) / middle)
    angles = times.astype(jnp.float32)[:, None] * freqs[None, :]
    return jnp.concatenate([jnp.cos(angles), jnp.sin(angles)], axis=1)


def norm_silu(values):
    count, height, width, chans = values.shape
    grouped = values.reshape(count, height, width, GROUPS, chans // GROUPS)
    center = jnp.mean(grouped, axis=(1, 2, 4), keepdims=True)
    spread = jnp.mean(jnp.square(grouped - center), axis=(1, 2, 4), keepdims=True)
    normed = ((grouped - center) * lax.rsqrt(spread + 1e-05)).reshape(values.shape)
    return jax.nn.silu(normed)


def patches(acts):
    height, width = (acts.shape[1], acts.shape[2])
    padded = jnp.pad(acts, ((0, 0), (1, 1), (1, 1), (0, 0)))
    taps = [
        padded[:, row_shift : row_shift + height, col_shift : col_shift + width, :]
        for row_shift in range(3)
        for col_shift in range(3)
    ]
    return jnp.concatenate(taps, axis=-1)


def conv_apply(acts, weights):
    cols = patches(acts)
    flat = cols.reshape(-1, cols.shape[-1])
    result = jnp.dot(flat, weights, preferred_element_type=jnp.float32)
    return result.reshape(acts.shape[:3] + (weights.shape[1],))


def conv_back(grads, weights):
    count, height, width, chans = grads.shape
    flat = grads.reshape(-1, chans)
    spread_back = jnp.dot(flat, weights.T, preferred_element_type=jnp.float32)
    in_chans = weights.shape[0] // 9
    spread_back = spread_back.reshape(count, height, width, 9, in_chans)
    padded = jnp.zeros((count, height + 2, width + 2, in_chans), jnp.float32)
    for index in range(9):
        row_shift, col_shift = (index // 3, index % 3)
        padded = padded.at[:, row_shift : row_shift + height, col_shift : col_shift + width, :].add(
            spread_back[:, :, :, index, :]
        )
    return padded[:, 1:-1, 1:-1, :]


def weight_grad(acts, grads):
    cols = patches(acts)
    flat = cols.reshape(-1, cols.shape[-1])
    return lax.dot_general(
        flat,
        grads.reshape(-1, grads.shape[-1]),
        (((0,), (0,)), ((), ())),
        preferred_element_type=jnp.float32,
    )


def section_forward(section_in, bias_rows, weight_one, weight_two):
    acts_one = norm_silu(section_in).astype(jnp.bfloat16)
    conv_mid = conv_apply(acts_one, weight_one) + bias_rows[:, None, None, :]
    acts_two = norm_silu(conv_mid).astype(jnp.bfloat16)
    return section_in + conv_apply(acts_two, weight_two)


def section_backward(section_in, bias_rows, weight_one, weight_two, grad_out):
    acts_one = norm_silu(section_in).astype(jnp.bfloat16)
    conv_mid = conv_apply(acts_one, weight_one) + bias_rows[:, None, None, :]
    acts_two = norm_silu(conv_mid).astype(jnp.bfloat16)
    grad_low = grad_out.astype(jnp.bfloat16)
    delta_two = weight_grad(acts_two, grad_low)
    grad_acts_two = conv_back(grad_low, weight_two)
    grad_mid = jax.vjp(norm_silu, conv_mid)[1](grad_acts_two)[0]
    grad_bias = jnp.sum(grad_mid, axis=(1, 2))
    grad_mid_low = grad_mid.astype(jnp.bfloat16)
    delta_one = weight_grad(acts_one, grad_mid_low)
    grad_acts_one = conv_back(grad_mid_low, weight_one)
    grad_in = grad_out + jax.vjp(norm_silu, section_in)[1](grad_acts_one)[0]
    return (grad_in, delta_one, delta_two, grad_bias)


def pick_slot(buffer, slot):
    return lax.dynamic_index_in_dim(buffer, slot, 0, keepdims=False)


def put_slot(buffer, slot, value, enabled):
    fresh = jnp.where(enabled, value, pick_slot(buffer, slot))
    return lax.dynamic_update_index_in_dim(buffer, fresh, slot, 0)


def local(features, target, timesteps, conv_one, conv_two, time_proj):
    sections = lax.axis_size("section")
    section_pos = lax.axis_index("section")
    middle = sections // 2
    partner = sections - 1 - section_pos
    is_decoder = section_pos >= middle
    is_encoder = section_pos < middle
    is_first = section_pos == 0
    is_last = section_pos == sections - 1
    images = features.shape[0] // MICRO
    row_len = WIDTH * CH
    weight_one = conv_one[0]
    weight_two = conv_two[0]
    embedded = embed_times(timesteps)
    bias_all = jnp.dot(embedded, time_proj[0], precision=lax.Precision.HIGHEST)
    feats_micro = features.reshape(MICRO, images, HEIGHT, row_len)
    target_micro = target.reshape(MICRO, images, HEIGHT, row_len)
    bias_micro = bias_all.reshape(MICRO, images, CH)
    embed_micro = embedded.reshape(MICRO, images, TE)
    tick_count = MICRO + sections - 1
    bit_count = sections.bit_length() - 1
    bit_list = list(range(bit_count))
    image_shape = (images, HEIGHT, WIDTH, CH)
    flat_shape = (images, HEIGHT, row_len)
    stack_shape = (middle,) + flat_shape
    scale = 1.0 / math.sqrt(HEIGHT * WIDTH)

    def route_forward(sent):
        moved = sent
        for bit in bit_list:
            moved = from_partner(moved, "section", bit)
        return moved

    def route_backward(sent):
        moved = sent
        for bit in bit_list:
            moved = from_partner(moved, "section", bit)
        return moved

    def forward_tick(carry, tick):
        incoming, skip_buffer, skip_stack, saved_inputs, last_outputs = carry
        micro_now = tick - section_pos
        active = (micro_now >= 0) & (micro_now < MICRO)
        slot = jnp.clip(micro_now, 0, MICRO - 1)
        given = jnp.where(is_first, pick_slot(feats_micro, slot).astype(jnp.float32), incoming)
        skip_now = pick_slot(skip_buffer, slot)
        skip_part = jnp.where(is_decoder, skip_now, 0.0)
        section_in = (given + skip_part).reshape(image_shape)
        bias_rows = pick_slot(bias_micro, slot)
        result = lax.cond(
            active,
            lambda: section_forward(section_in, bias_rows, weight_one, weight_two),
            lambda: jnp.zeros(image_shape, jnp.float32),
        )
        result = result.reshape(flat_shape)
        saved_inputs = put_slot(saved_inputs, slot, section_in, active)
        last_outputs = put_slot(last_outputs, slot, result, active & is_last)
        incoming = passed_along(result, "section", 1)
        arrived = route_forward(result)
        skip_micro = tick - partner
        usable = is_decoder & (skip_micro >= 0) & (skip_micro < MICRO)
        skip_slot = jnp.clip(skip_micro, 0, MICRO - 1)
        skip_buffer = put_slot(skip_buffer, skip_slot, arrived, usable)
        return ((incoming, skip_buffer, skip_stack, saved_inputs, last_outputs), None)

    start_fwd = (
        jnp.zeros(flat_shape, jnp.float32),
        jnp.zeros((MICRO,) + flat_shape, jnp.float32),
        jnp.zeros(stack_shape, jnp.float32),
        jnp.zeros((MICRO,) + image_shape, jnp.float32),
        jnp.zeros((MICRO,) + flat_shape, jnp.float32),
    )
    fwd_done, unused_out = lax.scan(forward_tick, start_fwd, jnp.arange(tick_count))
    saved_inputs, last_outputs = (fwd_done[3], fwd_done[4])

    def backward_tick(carry, tick):
        incoming, skip_grads, grad_stack, total_one, total_two, total_time = carry
        micro_now = tick - (sections - 1 - section_pos)
        active = (micro_now >= 0) & (micro_now < MICRO)
        slot = jnp.clip(micro_now, 0, MICRO - 1)
        loss_grad = (
            pick_slot(last_outputs, slot) - pick_slot(target_micro, slot).astype(jnp.float32)
        ) * scale
        given = jnp.where(is_last, loss_grad, incoming)
        skip_now = pick_slot(skip_grads, slot)
        given = given + jnp.where(is_encoder, skip_now, 0.0)
        grad_out = given.reshape(image_shape)
        section_in = pick_slot(saved_inputs, slot)
        bias_rows = pick_slot(bias_micro, slot)

        def run_section():
            return section_backward(section_in, bias_rows, weight_one, weight_two, grad_out)

        def quiet_section():
            return (
                jnp.zeros(image_shape, jnp.float32),
                jnp.zeros(weight_one.shape, jnp.float32),
                jnp.zeros(weight_two.shape, jnp.float32),
                jnp.zeros((images, CH), jnp.float32),
            )

        grad_in, delta_one, delta_two, grad_bias = lax.cond(active, run_section, quiet_section)
        delta_time = jnp.dot(
            pick_slot(embed_micro, slot).T, grad_bias, precision=lax.Precision.HIGHEST
        )
        grad_flat = grad_in.reshape(flat_shape)
        incoming = passed_along(grad_flat, "section", -1)
        arrived = route_backward(grad_flat)
        skip_micro = tick - section_pos
        usable = is_encoder & (skip_micro >= 0) & (skip_micro < MICRO)
        skip_slot = jnp.clip(skip_micro, 0, MICRO - 1)
        skip_grads = put_slot(skip_grads, skip_slot, arrived, usable)
        return (
            (
                incoming,
                skip_grads,
                grad_stack,
                total_one + delta_one,
                total_two + delta_two,
                total_time + delta_time,
            ),
            None,
        )

    start_bwd = (
        jnp.zeros(flat_shape, jnp.float32),
        jnp.zeros((MICRO,) + flat_shape, jnp.float32),
        jnp.zeros(stack_shape, jnp.float32),
        jnp.zeros(weight_one.shape, jnp.float32),
        jnp.zeros(weight_two.shape, jnp.float32),
        jnp.zeros((TE, CH), jnp.float32),
    )
    finished, unused_back = lax.scan(backward_tick, start_bwd, jnp.arange(tick_count))
    total_one, total_two, total_time = (finished[3], finished[4], finished[5])
    sum_one, sum_two, sum_time = lax.psum((total_one, total_two, total_time), "dp")
    return (sum_one[None], sum_two[None], sum_time[None])


PIX = HEIGHT * WIDTH
MESH_IDS = pl.DeviceIdType.MESH
VMEM_BYTES = 56 * 1024 * 1024
SUBLANES = 8


def group_mean(cols, same_group):
    wide = jnp.broadcast_to(cols, (8, CH))
    total = jnp.dot(
        wide, same_group, precision=lax.Precision.HIGHEST, preferred_element_type=jnp.float32
    )
    return total[0:1, :] * (1.0 / (PIX * (CH // GROUPS)))


def col_sum(values):
    return jnp.sum(values, axis=0, keepdims=True)


def norm_parts(values, same_group):
    centered = values - group_mean(col_sum(values), same_group)
    inv = lax.rsqrt(group_mean(col_sum(centered * centered), same_group) + 1e-05)
    normed = centered * inv
    gate = 1.0 / (1.0 + jnp.exp(-normed))
    return normed, gate, inv


def norm_back(parts, cotangent, same_group):
    normed, gate, inv = parts
    dn = cotangent * (gate * (1.0 + normed * (1.0 - gate)))
    mean_dn = group_mean(col_sum(dn), same_group)
    mean_dnn = group_mean(col_sum(dn * normed), same_group)
    return inv * (dn - mean_dn - normed * mean_dnn)


def side_taps(values):
    row = lax.broadcasted_iota(jnp.int32, (PIX, CH), 0) % HEIGHT
    before = jnp.where(row == 0, 0.0, pltpu.roll(values, 1, 0))
    after = jnp.where(row == HEIGHT - 1, 0.0, pltpu.roll(values, PIX - 1, 0))
    return before, values, after


def shifted(values, columns):
    edge = jnp.zeros((HEIGHT, values.shape[1]), values.dtype)
    if columns < 0:
        return jnp.concatenate([edge, values[: PIX - HEIGHT]], axis=0)
    if columns > 0:
        return jnp.concatenate([values[HEIGHT:], edge], axis=0)
    return values


def patch_rows(values):
    sides = [side.astype(jnp.bfloat16) for side in side_taps(values)]
    return jnp.concatenate([shifted(side, c) for side in sides for c in (-1, 0, 1)], axis=1)


def conv_rows_back(low, wt_ref):
    spread = jnp.dot(low, wt_ref[...], preferred_element_type=jnp.float32)
    rows = []
    for r in range(3):
        taps = [spread[:, (3 * r + c) * CH : (3 * r + c + 1) * CH] for c in range(3)]
        rows.append(shifted(taps[2], -1) + taps[1] + shifted(taps[0], 1))
    return side_taps(rows[2])[0] + rows[1] + side_taps(rows[0])[2]


def image_rows(ref, i):
    lines = ref[i].astype(jnp.float32)
    return jnp.concatenate([lines[:, w * CH : (w + 1) * CH] for w in range(WIDTH)], axis=0)


def activations(parts):
    normed, gate, _ = parts
    return patch_rows(normed * gate)


def group_matrix():
    assert CH // GROUPS == 10
    rows = lax.broadcasted_iota(jnp.int32, (CH, CH), 0) * 6554 >> 16
    cols = lax.broadcasted_iota(jnp.int32, (CH, CH), 1) * 6554 >> 16
    return jnp.where(rows == cols, 1.0, 0.0)


CORES = 2
CHIPS = 8
BLOCK = 2 * CH // (CORES * CHIPS)
SPLITS = tuple((first, 8) for first in range(0, BLOCK, 8))
SUBS = len(SPLITS)
LANES = 3072


def ring_places():
    dp = lax.axis_index("dp")
    core = dp % CORES
    chip = dp // CORES
    x, z = chip % 2, chip // 2
    place = z + x * (CHIPS - 1 - 2 * z)
    way = 1 - 2 * core

    def device(at):
        side = at // (CHIPS // 2)
        depth = at + side * (CHIPS - 1 - 2 * at)
        return {"dp": (depth * 2 + side) * CORES + core}

    after = device((place + way + CHIPS) % CHIPS)
    before = device((place - way + CHIPS) % CHIPS)
    sibling = {"dp": chip * CORES + 1 - core}
    return core, place, way, after, before, sibling


def greet(others):
    barrier = pltpu.get_barrier_semaphore()
    for other in others:
        pl.semaphore_signal(barrier, inc=1, device_id=other, device_id_type=MESH_IDS)


def await_greetings(count):
    pl.semaphore_wait(pltpu.get_barrier_semaphore(), count)


def ring_sum(places, in_ref, out_ref, pair_ref, slot_ref, work_ref, pair_sems, step_sems, turn_sems, give_sems):
    core, place, way, after, before, sibling = places

    def rows_of(half, block, sub):
        first, size = SPLITS[sub]
        start = (half * CHIPS + block) * BLOCK + first
        return pl.ds(pl.multiple_of(start, 8), size)

    def kept(ref, step, sub):
        first, size = SPLITS[sub]
        return ref.at[step, pl.ds(first, size)]

    def remote(src, dst, sems, index, target):
        return pltpu.make_async_remote_copy(
            src_ref=src,
            dst_ref=dst,
            send_sem=sems.at[(0,) + index],
            recv_sem=sems.at[(1,) + index],
            device_id=target,
            device_id_type=MESH_IDS,
        )

    def block_at(step):
        return (place - way * step + 2 * CHIPS) % CHIPS

    def sibling_block_at(step):
        return (place + way * step + 2 * CHIPS) % CHIPS

    pending = []
    pairs = {}
    for step in range(CHIPS):
        for sub in range(SUBS):
            theirs = sibling_block_at(step)
            copy = remote(
                in_ref.at[rows_of(1 - core, theirs, sub)], kept(pair_ref, step, sub), pair_sems, (step, sub), sibling
            )
            copy.start()
            pairs[step, sub] = copy
            pending.append(copy)

    arrived = {}
    for step in range(CHIPS):
        for sub in range(SUBS):
            block = block_at(step)
            pairs[step, sub].wait_recv()
            total = in_ref[rows_of(core, block, sub), :] + kept(pair_ref, step, sub)[...]
            if step:
                arrived[step - 1, sub].wait_recv()
                total = total + kept(slot_ref, step - 1, sub)[...]
            if step < CHIPS - 1:
                kept(work_ref, step, sub)[...] = total
                copy = remote(
                    kept(work_ref, step, sub), kept(slot_ref, step, sub), step_sems, (step, sub), after
                )
                copy.start()
                arrived[step, sub] = copy
                pending.append(copy)
            else:
                out_ref[rows_of(core, block, sub), :] = total

    turned = {}
    gifts = []
    for step in range(CHIPS):
        for sub in range(SUBS):
            block = block_at(CHIPS - 1 + step)
            if step:
                turned[step - 1, sub].wait_recv()
            here = out_ref.at[rows_of(core, block, sub)]
            if step < CHIPS - 1:
                copy = remote(here, here, turn_sems, (step, sub), after)
                copy.start()
                turned[step, sub] = copy
                pending.append(copy)
            copy = remote(here, here, give_sems, (step, sub), sibling)
            copy.start()
            gifts.append(copy)
    for copy in gifts:
        copy.wait_recv()
    for copy in pending + gifts:
        copy.wait_send()


def ring_scratch():
    return [
        pltpu.VMEM((CHIPS, BLOCK, LANES), jnp.float32),
        pltpu.VMEM((CHIPS - 1, BLOCK, LANES), jnp.float32),
        pltpu.VMEM((CHIPS - 1, BLOCK, LANES), jnp.float32),
        pltpu.SemaphoreType.DMA((2, CHIPS, SUBS)),
        pltpu.SemaphoreType.DMA((2, CHIPS - 1, SUBS)),
        pltpu.SemaphoreType.DMA((2, CHIPS - 1, SUBS)),
        pltpu.SemaphoreType.DMA((2, CHIPS, SUBS)),
    ]


def whole_kernel(
    x_ref, target_ref, emb_ref, proj_ref, wt1_ref, wt2_ref,
    out_ref, same_ref, bias_ref, dbias_ref, w1_ref, w2_ref, taps1_ref, taps2_ref, low1_ref, low2_ref,
    mid_ref, send_ref, inbox_ref, buf_ref, send_sems, recv_sems, *ring_refs
):
    section = lax.axis_index("section")
    places = ring_places()
    partner = {"section": 1 - section}
    others = places[3:] + (partner,)
    greet(others)
    images = x_ref.shape[0]
    highest = lax.Precision.HIGHEST
    same_ref[...] = group_matrix()
    bias_ref[...] = jnp.dot(
        emb_ref[...], proj_ref[0], precision=highest, preferred_element_type=jnp.float32
    )
    dbias_ref[...] = jnp.zeros_like(dbias_ref)
    w1_ref[...] = wt1_ref[...].T
    w2_ref[...] = wt2_ref[...].T
    await_greetings(len(others))

    def sent(i):
        return pltpu.make_async_remote_copy(
            src_ref=send_ref.at[i],
            dst_ref=inbox_ref.at[i],
            send_sem=send_sems.at[i],
            recv_sem=recv_sems.at[i],
            device_id=partner,
            device_id_type=MESH_IDS,
        )

    def rows_of(i):
        return pl.ds(pl.multiple_of(i * PIX, PIX), PIX)

    def forward(i, rows, same):
        parts_a = norm_parts(rows, same)
        taps = activations(parts_a)
        taps1_ref[rows_of(i), :] = taps
        mid = jnp.dot(taps, w1_ref[...], preferred_element_type=jnp.float32)
        mid = mid + bias_ref[pl.ds(i, 1), :]
        parts_b = norm_parts(mid, same)
        taps = activations(parts_b)
        taps2_ref[rows_of(i), :] = taps
        out = rows + jnp.dot(taps, w2_ref[...], preferred_element_type=jnp.float32)
        return mid, out, parts_a, parts_b

    def backward_to_mid(i, grad, parts_b, same):
        low = grad.astype(jnp.bfloat16)
        low2_ref[rows_of(i), :] = low
        grad_mid = norm_back(parts_b, conv_rows_back(low, wt2_ref), same)
        dbias_ref[pl.ds(i, 1), :] = col_sum(grad_mid)
        low = grad_mid.astype(jnp.bfloat16)
        low1_ref[rows_of(i), :] = low
        return low

    @pl.when(section == 0)
    def _():
        @pl.loop(0, images)
        def _(i):
            mid, out, *_ = forward(i, image_rows(x_ref, i), same_ref[...])
            mid_ref[i] = mid
            send_ref[i] = out
            sent(i).start()

        @pl.loop(0, images)
        def _(i):
            same = same_ref[...]
            parts_b = norm_parts(mid_ref[i], same)
            sent(i).wait_recv()
            backward_to_mid(i, inbox_ref[i] + inbox_ref[i], parts_b, same)

    @pl.when(section == 1)
    def _():
        @pl.loop(0, images)
        def _(i):
            same = same_ref[...]
            wanted = image_rows(target_ref, i)
            sent(i).wait_recv()
            _, out, parts_a, parts_b = forward(i, inbox_ref[i] + inbox_ref[i], same)
            grad = (out - wanted) * (1.0 / math.sqrt(PIX))
            low = backward_to_mid(i, grad, parts_b, same)
            send_ref[i] = grad + norm_back(parts_a, conv_rows_back(low, wt1_ref), same)
            sent(i).start()

    for first, low_ref, taps_ref in ((CH, low2_ref, taps2_ref), (0, low1_ref, taps1_ref)):
        buf_ref[first : first + CH, : 9 * CH] = jnp.dot(
            low_ref[...].T, taps_ref[...], preferred_element_type=jnp.float32
        )
    d_time = jnp.dot(
        emb_ref[...].T, dbias_ref[...], precision=highest, preferred_element_type=jnp.float32
    )
    half = CH // 2
    blank = jnp.zeros((TE, LANES - 9 * CH - half), jnp.float32)
    buf_ref[:TE, 9 * CH :] = jnp.concatenate([d_time[:, :half], blank], axis=1)
    buf_ref[TE:, 9 * CH :] = jnp.concatenate([d_time[:, half:], blank], axis=1)
    for i in range(images):
        sent(i).wait_send()
    ring_sum(places, buf_ref, out_ref, *ring_refs)


def unpack_kernel(one_in, two_in, one_ref, two_ref, time_ref):
    half = CH // 2
    one_ref[...] = one_in[:, : 9 * CH]
    two_ref[...] = two_in[:, : 9 * CH]
    time_ref[...] = jnp.concatenate(
        [one_in[:, 9 * CH : 9 * CH + half], two_in[:, 9 * CH : 9 * CH + half]], axis=1
    )


def local_two(features, target, timesteps, conv_one, conv_two, time_proj):
    images = features.shape[0]
    emb_rows = -(-images // SUBLANES) * SUBLANES
    embedded = embed_times(jnp.pad(timesteps, (0, emb_rows - images)))
    stack = pltpu.VMEM((images, PIX, CH), jnp.float32)
    weight = pltpu.VMEM((9 * CH, CH), jnp.bfloat16)
    taps = pltpu.VMEM((images * PIX, 9 * CH), jnp.bfloat16)
    low = pltpu.VMEM((images * PIX, CH), jnp.bfloat16)
    row = pltpu.VMEM((emb_rows, CH), jnp.float32)
    total = pl.pallas_call(
        whole_kernel,
        name="whole",
        out_shape=jax.ShapeDtypeStruct((2 * CH, LANES), jnp.float32),
        in_specs=[pl.BlockSpec(memory_space=pltpu.VMEM)] * 6,
        out_specs=pl.BlockSpec(memory_space=pltpu.VMEM),
        scratch_shapes=[
            pltpu.VMEM((CH, CH), jnp.float32),
            row,
            row,
            weight,
            weight,
            taps,
            taps,
            low,
            low,
            stack,
            stack,
            stack,
            pltpu.VMEM((2 * CH, LANES), jnp.float32),
            pltpu.SemaphoreType.DMA((images,)),
            pltpu.SemaphoreType.DMA((images,)),
        ]
        + ring_scratch(),
        compiler_params=pltpu.CompilerParams(
            collective_id=0, has_side_effects=True, vmem_limit_bytes=VMEM_BYTES
        ),
    )(features, target, embedded, time_proj, conv_one[0].T, conv_two[0].T)
    step = 64
    steps = CH // step
    grad = jax.ShapeDtypeStruct((CH, 9 * CH), jnp.float32)
    one, two, d_time = pl.pallas_call(
        unpack_kernel,
        name="unpack",
        grid=(steps,),
        in_specs=[
            pl.BlockSpec((step, LANES), lambda i: (i, 0)),
            pl.BlockSpec((step, LANES), lambda i: (i + steps, 0)),
        ],
        out_specs=[
            pl.BlockSpec((step, 9 * CH), lambda i: (i, 0)),
            pl.BlockSpec((step, 9 * CH), lambda i: (i, 0)),
            pl.BlockSpec((step, CH), lambda i: (i, 0)),
        ],
        out_shape=[grad, grad, jax.ShapeDtypeStruct((TE, CH), jnp.float32)],
    )(total, total)
    return (one.T[None], two.T[None], d_time[None])


def solution(mesh):
    placed = (
        P("dp", None, None),
        P("dp", None, None),
        P("dp"),
        P("section", None, None),
        P("section", None, None),
        P("section", None, None),
    )
    two = mesh.shape["section"] == 2 and mesh.shape["dp"] == CORES * CHIPS
    body = local_two if two else local
    return jax.shard_map(
        body,
        mesh=mesh,
        in_specs=placed,
        out_specs=(P("section", None, None), P("section", None, None), P("section", None, None)),
        check_vma=False,
    )
```

```python
import math

import jax
import jax.numpy as jnp
from jax import lax
from jax.experimental import pallas as pl
from jax.experimental.pallas import tpu as pltpu
from jax.sharding import PartitionSpec as P

CH = 320
TE = 320
GROUPS = 32
HEIGHT = 16
WIDTH = 16
MICRO = 2


def from_partner(value, axis, apart):
    mask = 2**apart
    pairs = [(source, source ^ mask) for source in range(lax.axis_size(axis))]
    return lax.ppermute(value, axis, pairs)


def passed_along(block, axis, distance):
    devices = range(lax.axis_size(axis))
    route = [(i - distance, i) for i in devices if i - distance in devices]
    return lax.ppermute(block, axis, route)


def embed_times(times):
    middle = TE // 2
    freqs = jnp.exp(-math.log(10000.0) * jnp.arange(middle, dtype=jnp.float32) / middle)
    angles = times.astype(jnp.float32)[:, None] * freqs[None, :]
    return jnp.concatenate([jnp.cos(angles), jnp.sin(angles)], axis=1)


def norm_silu(values):
    count, height, width, chans = values.shape
    grouped = values.reshape(count, height, width, GROUPS, chans // GROUPS)
    center = jnp.mean(grouped, axis=(1, 2, 4), keepdims=True)
    spread = jnp.mean(jnp.square(grouped - center), axis=(1, 2, 4), keepdims=True)
    normed = ((grouped - center) * lax.rsqrt(spread + 1e-05)).reshape(values.shape)
    return jax.nn.silu(normed)


def patches(acts):
    height, width = (acts.shape[1], acts.shape[2])
    padded = jnp.pad(acts, ((0, 0), (1, 1), (1, 1), (0, 0)))
    taps = [
        padded[:, row_shift : row_shift + height, col_shift : col_shift + width, :]
        for row_shift in range(3)
        for col_shift in range(3)
    ]
    return jnp.concatenate(taps, axis=-1)


def conv_apply(acts, weights):
    cols = patches(acts)
    flat = cols.reshape(-1, cols.shape[-1])
    result = jnp.dot(flat, weights, preferred_element_type=jnp.float32)
    return result.reshape(acts.shape[:3] + (weights.shape[1],))


def conv_back(grads, weights):
    count, height, width, chans = grads.shape
    flat = grads.reshape(-1, chans)
    spread_back = jnp.dot(flat, weights.T, preferred_element_type=jnp.float32)
    in_chans = weights.shape[0] // 9
    spread_back = spread_back.reshape(count, height, width, 9, in_chans)
    padded = jnp.zeros((count, height + 2, width + 2, in_chans), jnp.float32)
    for index in range(9):
        row_shift, col_shift = (index // 3, index % 3)
        padded = padded.at[:, row_shift : row_shift + height, col_shift : col_shift + width, :].add(
            spread_back[:, :, :, index, :]
        )
    return padded[:, 1:-1, 1:-1, :]


def weight_grad(acts, grads):
    cols = patches(acts)
    flat = cols.reshape(-1, cols.shape[-1])
    return lax.dot_general(
        flat,
        grads.reshape(-1, grads.shape[-1]),
        (((0,), (0,)), ((), ())),
        preferred_element_type=jnp.float32,
    )


def section_forward(section_in, bias_rows, weight_one, weight_two):
    acts_one = norm_silu(section_in).astype(jnp.bfloat16)
    conv_mid = conv_apply(acts_one, weight_one) + bias_rows[:, None, None, :]
    acts_two = norm_silu(conv_mid).astype(jnp.bfloat16)
    return section_in + conv_apply(acts_two, weight_two)


def section_backward(section_in, bias_rows, weight_one, weight_two, grad_out):
    acts_one = norm_silu(section_in).astype(jnp.bfloat16)
    conv_mid = conv_apply(acts_one, weight_one) + bias_rows[:, None, None, :]
    acts_two = norm_silu(conv_mid).astype(jnp.bfloat16)
    grad_low = grad_out.astype(jnp.bfloat16)
    delta_two = weight_grad(acts_two, grad_low)
    grad_acts_two = conv_back(grad_low, weight_two)
    grad_mid = jax.vjp(norm_silu, conv_mid)[1](grad_acts_two)[0]
    grad_bias = jnp.sum(grad_mid, axis=(1, 2))
    grad_mid_low = grad_mid.astype(jnp.bfloat16)
    delta_one = weight_grad(acts_one, grad_mid_low)
    grad_acts_one = conv_back(grad_mid_low, weight_one)
    grad_in = grad_out + jax.vjp(norm_silu, section_in)[1](grad_acts_one)[0]
    return (grad_in, delta_one, delta_two, grad_bias)


def pick_slot(buffer, slot):
    return lax.dynamic_index_in_dim(buffer, slot, 0, keepdims=False)


def put_slot(buffer, slot, value, enabled):
    fresh = jnp.where(enabled, value, pick_slot(buffer, slot))
    return lax.dynamic_update_index_in_dim(buffer, fresh, slot, 0)


def local(features, target, timesteps, conv_one, conv_two, time_proj):
    sections = lax.axis_size("section")
    section_pos = lax.axis_index("section")
    middle = sections // 2
    partner = sections - 1 - section_pos
    is_decoder = section_pos >= middle
    is_encoder = section_pos < middle
    is_first = section_pos == 0
    is_last = section_pos == sections - 1
    images = features.shape[0] // MICRO
    row_len = WIDTH * CH
    weight_one = conv_one[0]
    weight_two = conv_two[0]
    embedded = embed_times(timesteps)
    bias_all = jnp.dot(embedded, time_proj[0], precision=lax.Precision.HIGHEST)
    feats_micro = features.reshape(MICRO, images, HEIGHT, row_len)
    target_micro = target.reshape(MICRO, images, HEIGHT, row_len)
    bias_micro = bias_all.reshape(MICRO, images, CH)
    embed_micro = embedded.reshape(MICRO, images, TE)
    tick_count = MICRO + sections - 1
    bit_count = sections.bit_length() - 1
    bit_list = list(range(bit_count))
    image_shape = (images, HEIGHT, WIDTH, CH)
    flat_shape = (images, HEIGHT, row_len)
    stack_shape = (middle,) + flat_shape
    scale = 1.0 / math.sqrt(HEIGHT * WIDTH)

    def route_forward(sent):
        moved = sent
        for bit in bit_list:
            moved = from_partner(moved, "section", bit)
        return moved

    def route_backward(sent):
        moved = sent
        for bit in bit_list:
            moved = from_partner(moved, "section", bit)
        return moved

    def forward_tick(carry, tick):
        incoming, skip_buffer, skip_stack, saved_inputs, last_outputs = carry
        micro_now = tick - section_pos
        active = (micro_now >= 0) & (micro_now < MICRO)
        slot = jnp.clip(micro_now, 0, MICRO - 1)
        given = jnp.where(is_first, pick_slot(feats_micro, slot).astype(jnp.float32), incoming)
        skip_now = pick_slot(skip_buffer, slot)
        skip_part = jnp.where(is_decoder, skip_now, 0.0)
        section_in = (given + skip_part).reshape(image_shape)
        bias_rows = pick_slot(bias_micro, slot)
        result = lax.cond(
            active,
            lambda: section_forward(section_in, bias_rows, weight_one, weight_two),
            lambda: jnp.zeros(image_shape, jnp.float32),
        )
        result = result.reshape(flat_shape)
        saved_inputs = put_slot(saved_inputs, slot, section_in, active)
        last_outputs = put_slot(last_outputs, slot, result, active & is_last)
        incoming = passed_along(result, "section", 1)
        arrived = route_forward(result)
        skip_micro = tick - partner
        usable = is_decoder & (skip_micro >= 0) & (skip_micro < MICRO)
        skip_slot = jnp.clip(skip_micro, 0, MICRO - 1)
        skip_buffer = put_slot(skip_buffer, skip_slot, arrived, usable)
        return ((incoming, skip_buffer, skip_stack, saved_inputs, last_outputs), None)

    start_fwd = (
        jnp.zeros(flat_shape, jnp.float32),
        jnp.zeros((MICRO,) + flat_shape, jnp.float32),
        jnp.zeros(stack_shape, jnp.float32),
        jnp.zeros((MICRO,) + image_shape, jnp.float32),
        jnp.zeros((MICRO,) + flat_shape, jnp.float32),
    )
    fwd_done, unused_out = lax.scan(forward_tick, start_fwd, jnp.arange(tick_count))
    saved_inputs, last_outputs = (fwd_done[3], fwd_done[4])

    def backward_tick(carry, tick):
        incoming, skip_grads, grad_stack, total_one, total_two, total_time = carry
        micro_now = tick - (sections - 1 - section_pos)
        active = (micro_now >= 0) & (micro_now < MICRO)
        slot = jnp.clip(micro_now, 0, MICRO - 1)
        loss_grad = (
            pick_slot(last_outputs, slot) - pick_slot(target_micro, slot).astype(jnp.float32)
        ) * scale
        given = jnp.where(is_last, loss_grad, incoming)
        skip_now = pick_slot(skip_grads, slot)
        given = given + jnp.where(is_encoder, skip_now, 0.0)
        grad_out = given.reshape(image_shape)
        section_in = pick_slot(saved_inputs, slot)
        bias_rows = pick_slot(bias_micro, slot)

        def run_section():
            return section_backward(section_in, bias_rows, weight_one, weight_two, grad_out)

        def quiet_section():
            return (
                jnp.zeros(image_shape, jnp.float32),
                jnp.zeros(weight_one.shape, jnp.float32),
                jnp.zeros(weight_two.shape, jnp.float32),
                jnp.zeros((images, CH), jnp.float32),
            )

        grad_in, delta_one, delta_two, grad_bias = lax.cond(active, run_section, quiet_section)
        delta_time = jnp.dot(
            pick_slot(embed_micro, slot).T, grad_bias, precision=lax.Precision.HIGHEST
        )
        grad_flat = grad_in.reshape(flat_shape)
        incoming = passed_along(grad_flat, "section", -1)
        arrived = route_backward(grad_flat)
        skip_micro = tick - section_pos
        usable = is_encoder & (skip_micro >= 0) & (skip_micro < MICRO)
        skip_slot = jnp.clip(skip_micro, 0, MICRO - 1)
        skip_grads = put_slot(skip_grads, skip_slot, arrived, usable)
        return (
            (
                incoming,
                skip_grads,
                grad_stack,
                total_one + delta_one,
                total_two + delta_two,
                total_time + delta_time,
            ),
            None,
        )

    start_bwd = (
        jnp.zeros(flat_shape, jnp.float32),
        jnp.zeros((MICRO,) + flat_shape, jnp.float32),
        jnp.zeros(stack_shape, jnp.float32),
        jnp.zeros(weight_one.shape, jnp.float32),
        jnp.zeros(weight_two.shape, jnp.float32),
        jnp.zeros((TE, CH), jnp.float32),
    )
    finished, unused_back = lax.scan(backward_tick, start_bwd, jnp.arange(tick_count))
    total_one, total_two, total_time = (finished[3], finished[4], finished[5])
    sum_one, sum_two, sum_time = lax.psum((total_one, total_two, total_time), "dp")
    return (sum_one[None], sum_two[None], sum_time[None])


PIX = HEIGHT * WIDTH
MESH_IDS = pl.DeviceIdType.MESH
VMEM_BYTES = 56 * 1024 * 1024
SUBLANES = 8


def group_mean(cols, same_group):
    wide = jnp.broadcast_to(cols, (8, CH))
    total = jnp.dot(
        wide, same_group, precision=lax.Precision.HIGHEST, preferred_element_type=jnp.float32
    )
    return total[0:1, :] * (1.0 / (PIX * (CH // GROUPS)))


def col_sum(values):
    return jnp.sum(values, axis=0, keepdims=True)


def norm_parts(values, same_group):
    centered = values - group_mean(col_sum(values), same_group)
    inv = lax.rsqrt(group_mean(col_sum(centered * centered), same_group) + 1e-05)
    normed = centered * inv
    gate = 1.0 / (1.0 + jnp.exp(-normed))
    return normed, gate, inv


def norm_back(parts, cotangent, same_group):
    normed, gate, inv = parts
    dn = cotangent * (gate * (1.0 + normed * (1.0 - gate)))
    mean_dn = group_mean(col_sum(dn), same_group)
    mean_dnn = group_mean(col_sum(dn * normed), same_group)
    return inv * (dn - mean_dn - normed * mean_dnn)


def side_taps(values):
    row = lax.broadcasted_iota(jnp.int32, (PIX, CH), 0) % HEIGHT
    before = jnp.where(row == 0, 0.0, pltpu.roll(values, 1, 0))
    after = jnp.where(row == HEIGHT - 1, 0.0, pltpu.roll(values, PIX - 1, 0))
    return before, values, after


def shifted(values, columns):
    edge = jnp.zeros((HEIGHT, values.shape[1]), values.dtype)
    if columns < 0:
        return jnp.concatenate([edge, values[: PIX - HEIGHT]], axis=0)
    if columns > 0:
        return jnp.concatenate([values[HEIGHT:], edge], axis=0)
    return values


def patch_rows(values):
    sides = [side.astype(jnp.bfloat16) for side in side_taps(values)]
    return jnp.concatenate([shifted(side, c) for side in sides for c in (-1, 0, 1)], axis=1)


def conv_rows_back(low, wt_ref):
    spread = jnp.dot(low, wt_ref[...], preferred_element_type=jnp.float32)
    rows = []
    for r in range(3):
        taps = [spread[:, (3 * r + c) * CH : (3 * r + c + 1) * CH] for c in range(3)]
        rows.append(shifted(taps[2], -1) + taps[1] + shifted(taps[0], 1))
    return side_taps(rows[2])[0] + rows[1] + side_taps(rows[0])[2]


def image_rows(ref, i):
    lines = ref[i].astype(jnp.float32)
    return jnp.concatenate([lines[:, w * CH : (w + 1) * CH] for w in range(WIDTH)], axis=0)


def activations(parts):
    normed, gate, _ = parts
    return patch_rows(normed * gate)


def group_matrix():
    assert CH // GROUPS == 10
    rows = lax.broadcasted_iota(jnp.int32, (CH, CH), 0) * 6554 >> 16
    cols = lax.broadcasted_iota(jnp.int32, (CH, CH), 1) * 6554 >> 16
    return jnp.where(rows == cols, 1.0, 0.0)


CORES = 2
CHIPS = 8
BLOCK = 2 * CH // (CORES * CHIPS)
SPLITS = tuple((first, 8) for first in range(0, BLOCK, 8))
SUBS = len(SPLITS)
LANES = 3072


def ring_places():
    dp = lax.axis_index("dp")
    core = dp % CORES
    chip = dp // CORES
    x, z = chip % 2, chip // 2
    place = z + x * (CHIPS - 1 - 2 * z)
    way = 1 - 2 * core

    def device(at):
        side = at // (CHIPS // 2)
        depth = at + side * (CHIPS - 1 - 2 * at)
        return {"dp": (depth * 2 + side) * CORES + core}

    after = device((place + way + CHIPS) % CHIPS)
    before = device((place - way + CHIPS) % CHIPS)
    sibling = {"dp": chip * CORES + 1 - core}
    return core, place, way, after, before, sibling


def greet(others):
    barrier = pltpu.get_barrier_semaphore()
    for other in others:
        pl.semaphore_signal(barrier, inc=1, device_id=other, device_id_type=MESH_IDS)


def await_greetings(count):
    pl.semaphore_wait(pltpu.get_barrier_semaphore(), count)


def ring_sum(places, in_ref, out_ref, pair_ref, slot_ref, work_ref, pair_sems, step_sems, turn_sems, give_sems, keep_sems):
    core, place, way, after, before, sibling = places

    def rows_of(half, block, sub):
        first, size = SPLITS[sub]
        start = (half * CHIPS + block) * BLOCK + first
        return pl.ds(pl.multiple_of(start, 8), size)

    def kept(ref, step, sub):
        first, size = SPLITS[sub]
        return ref.at[step, pl.ds(first, size)]

    def remote(src, dst, sems, index, target):
        return pltpu.make_async_remote_copy(
            src_ref=src,
            dst_ref=dst,
            send_sem=sems.at[(0,) + index],
            recv_sem=sems.at[(1,) + index],
            device_id=target,
            device_id_type=MESH_IDS,
        )

    def block_at(step):
        return (place - way * step + 2 * CHIPS) % CHIPS

    def sibling_block_at(step):
        return (place + way * step + 2 * CHIPS) % CHIPS

    pending = []
    pairs = {}
    for step in range(CHIPS):
        for sub in range(SUBS):
            theirs = sibling_block_at(step)
            copy = remote(
                in_ref.at[rows_of(1 - core, theirs, sub)], kept(pair_ref, step, sub), pair_sems, (step, sub), sibling
            )
            copy.start()
            pairs[step, sub] = copy
            pending.append(copy)

    arrived = {}
    for step in range(CHIPS):
        for sub in range(SUBS):
            block = block_at(step)
            pairs[step, sub].wait_recv()
            total = in_ref[rows_of(core, block, sub), :] + kept(pair_ref, step, sub)[...]
            if step:
                arrived[step - 1, sub].wait_recv()
                total = total + kept(slot_ref, step - 1, sub)[...]
            if step < CHIPS - 1:
                kept(work_ref, step, sub)[...] = total
                copy = remote(
                    kept(work_ref, step, sub), kept(slot_ref, step, sub), step_sems, (step, sub), after
                )
                copy.start()
                arrived[step, sub] = copy
                pending.append(copy)
            else:
                kept(work_ref, step, sub)[...] = total

    turned = {}
    gifts = []
    stays = []
    for step in range(CHIPS):
        for sub in range(SUBS):
            block = block_at(CHIPS - 1 + step)
            if step:
                turned[step - 1, sub].wait_recv()
            here = out_ref.at[rows_of(core, block, sub)]
            held = here if step else kept(work_ref, CHIPS - 1, sub)
            if step == 0:
                copy = pltpu.make_async_copy(held, here, keep_sems.at[sub])
                copy.start()
                stays.append(copy)
            if step < CHIPS - 1:
                copy = remote(held, here, turn_sems, (step, sub), after)
                copy.start()
                turned[step, sub] = copy
                pending.append(copy)
            copy = remote(held, here, give_sems, (step, sub), sibling)
            copy.start()
            gifts.append(copy)
    for copy in stays:
        copy.wait()
    for copy in gifts:
        copy.wait_recv()
    for copy in pending + gifts:
        copy.wait_send()


def ring_scratch():
    return [
        pltpu.VMEM((CHIPS, BLOCK, LANES), jnp.float32),
        pltpu.VMEM((CHIPS - 1, BLOCK, LANES), jnp.float32),
        pltpu.VMEM((CHIPS, BLOCK, LANES), jnp.float32),
        pltpu.SemaphoreType.DMA((2, CHIPS, SUBS)),
        pltpu.SemaphoreType.DMA((2, CHIPS - 1, SUBS)),
        pltpu.SemaphoreType.DMA((2, CHIPS - 1, SUBS)),
        pltpu.SemaphoreType.DMA((2, CHIPS, SUBS)),
        pltpu.SemaphoreType.DMA((SUBS,)),
    ]


def whole_kernel(
    x_ref, target_ref, emb_ref, proj_ref, wt1_hbm, wt2_hbm,
    out_ref, same_ref, bias_ref, dbias_ref, w1_ref, w2_ref, taps1_ref, taps2_ref, low1_ref, low2_ref,
    mid_ref, send_ref, inbox_ref, buf_ref, wt1_ref, wt2_ref, load_sems, send_sems, recv_sems, *ring_refs
):
    load_one = pltpu.make_async_copy(wt1_hbm, wt1_ref, load_sems.at[0])
    load_two = pltpu.make_async_copy(wt2_hbm, wt2_ref, load_sems.at[1])
    load_one.start()
    load_two.start()
    section = lax.axis_index("section")
    places = ring_places()
    partner = {"section": 1 - section}
    others = places[3:] + (partner,)
    greet(others)
    images = x_ref.shape[0]
    highest = lax.Precision.HIGHEST
    same_ref[...] = group_matrix()
    bias_ref[...] = jnp.dot(
        emb_ref[...], proj_ref[0], precision=highest, preferred_element_type=jnp.float32
    )
    dbias_ref[...] = jnp.zeros_like(dbias_ref)
    load_one.wait()
    w1_ref[...] = wt1_ref[...].T
    load_two.wait()
    w2_ref[...] = wt2_ref[...].T
    await_greetings(len(others))

    def sent(i):
        return pltpu.make_async_remote_copy(
            src_ref=send_ref.at[i],
            dst_ref=inbox_ref.at[i],
            send_sem=send_sems.at[i],
            recv_sem=recv_sems.at[i],
            device_id=partner,
            device_id_type=MESH_IDS,
        )

    def rows_of(i):
        return pl.ds(pl.multiple_of(i * PIX, PIX), PIX)

    def forward(i, rows, same):
        parts_a = norm_parts(rows, same)
        taps = activations(parts_a)
        taps1_ref[rows_of(i), :] = taps
        mid = jnp.dot(taps, w1_ref[...], preferred_element_type=jnp.float32)
        mid = mid + bias_ref[pl.ds(i, 1), :]
        parts_b = norm_parts(mid, same)
        taps = activations(parts_b)
        taps2_ref[rows_of(i), :] = taps
        out = rows + jnp.dot(taps, w2_ref[...], preferred_element_type=jnp.float32)
        return mid, out, parts_a, parts_b

    def backward_to_mid(i, grad, parts_b, same):
        low = grad.astype(jnp.bfloat16)
        low2_ref[rows_of(i), :] = low
        grad_mid = norm_back(parts_b, conv_rows_back(low, wt2_ref), same)
        dbias_ref[pl.ds(i, 1), :] = col_sum(grad_mid)
        low = grad_mid.astype(jnp.bfloat16)
        low1_ref[rows_of(i), :] = low
        return low

    @pl.when(section == 0)
    def _():
        @pl.loop(0, images)
        def _(i):
            mid, out, *_ = forward(i, image_rows(x_ref, i), same_ref[...])
            mid_ref[i] = mid
            send_ref[i] = out
            sent(i).start()

        @pl.loop(0, images)
        def _(i):
            same = same_ref[...]
            parts_b = norm_parts(mid_ref[i], same)
            sent(i).wait_recv()
            backward_to_mid(i, inbox_ref[i] + inbox_ref[i], parts_b, same)

    @pl.when(section == 1)
    def _():
        @pl.loop(0, images)
        def _(i):
            same = same_ref[...]
            wanted = image_rows(target_ref, i)
            sent(i).wait_recv()
            _, out, parts_a, parts_b = forward(i, inbox_ref[i] + inbox_ref[i], same)
            grad = (out - wanted) * (1.0 / math.sqrt(PIX))
            low = backward_to_mid(i, grad, parts_b, same)
            send_ref[i] = grad + norm_back(parts_a, conv_rows_back(low, wt1_ref), same)
            sent(i).start()

    for first, low_ref, taps_ref in ((CH, low2_ref, taps2_ref), (0, low1_ref, taps1_ref)):
        buf_ref[first : first + CH, : 9 * CH] = jnp.dot(
            low_ref[...].T, taps_ref[...], preferred_element_type=jnp.float32
        )
    d_time = jnp.dot(
        emb_ref[...].T, dbias_ref[...], precision=highest, preferred_element_type=jnp.float32
    )
    half = CH // 2
    blank = jnp.zeros((TE, LANES - 9 * CH - half), jnp.float32)
    buf_ref[:TE, 9 * CH :] = jnp.concatenate([d_time[:, :half], blank], axis=1)
    buf_ref[TE:, 9 * CH :] = jnp.concatenate([d_time[:, half:], blank], axis=1)
    for i in range(images):
        sent(i).wait_send()
    ring_sum(places, buf_ref, out_ref, *ring_refs)


def unpack_kernel(one_in, two_in, one_ref, two_ref, time_ref):
    half = CH // 2
    one_ref[...] = one_in[:, : 9 * CH]
    two_ref[...] = two_in[:, : 9 * CH]
    time_ref[...] = jnp.concatenate(
        [one_in[:, 9 * CH : 9 * CH + half], two_in[:, 9 * CH : 9 * CH + half]], axis=1
    )


def local_two(features, target, timesteps, conv_one, conv_two, time_proj):
    images = features.shape[0]
    emb_rows = -(-images // SUBLANES) * SUBLANES
    embedded = embed_times(jnp.pad(timesteps, (0, emb_rows - images)))
    stack = pltpu.VMEM((images, PIX, CH), jnp.float32)
    weight = pltpu.VMEM((9 * CH, CH), jnp.bfloat16)
    taps = pltpu.VMEM((images * PIX, 9 * CH), jnp.bfloat16)
    low = pltpu.VMEM((images * PIX, CH), jnp.bfloat16)
    row = pltpu.VMEM((emb_rows, CH), jnp.float32)
    total = pl.pallas_call(
        whole_kernel,
        name="whole",
        out_shape=jax.ShapeDtypeStruct((2 * CH, LANES), jnp.float32),
        in_specs=[pl.BlockSpec(memory_space=pltpu.VMEM)] * 4
        + [pl.BlockSpec(memory_space=pl.ANY)] * 2,
        out_specs=pl.BlockSpec(memory_space=pl.ANY),
        scratch_shapes=[
            pltpu.VMEM((CH, CH), jnp.float32),
            row,
            row,
            weight,
            weight,
            taps,
            taps,
            low,
            low,
            stack,
            stack,
            stack,
            pltpu.VMEM((2 * CH, LANES), jnp.float32),
            pltpu.VMEM((CH, 9 * CH), jnp.bfloat16),
            pltpu.VMEM((CH, 9 * CH), jnp.bfloat16),
            pltpu.SemaphoreType.DMA((2,)),
            pltpu.SemaphoreType.DMA((images,)),
            pltpu.SemaphoreType.DMA((images,)),
        ]
        + ring_scratch(),
        compiler_params=pltpu.CompilerParams(
            collective_id=0, has_side_effects=True, vmem_limit_bytes=VMEM_BYTES
        ),
    )(features, target, embedded, time_proj, conv_one[0].T, conv_two[0].T)
    step = 64
    steps = CH // step
    grad = jax.ShapeDtypeStruct((CH, 9 * CH), jnp.float32)
    one, two, d_time = pl.pallas_call(
        unpack_kernel,
        name="unpack",
        grid=(steps,),
        in_specs=[
            pl.BlockSpec((step, LANES), lambda i: (i, 0)),
            pl.BlockSpec((step, LANES), lambda i: (i + steps, 0)),
        ],
        out_specs=[
            pl.BlockSpec((step, 9 * CH), lambda i: (i, 0)),
            pl.BlockSpec((step, 9 * CH), lambda i: (i, 0)),
            pl.BlockSpec((step, CH), lambda i: (i, 0)),
        ],
        out_shape=[grad, grad, jax.ShapeDtypeStruct((TE, CH), jnp.float32)],
    )(total, total)
    return (one.T[None], two.T[None], d_time[None])


def solution(mesh):
    placed = (
        P("dp", None, None),
        P("dp", None, None),
        P("dp"),
        P("section", None, None),
        P("section", None, None),
        P("section", None, None),
    )
    two = mesh.shape["section"] == 2 and mesh.shape["dp"] == CORES * CHIPS
    body = local_two if two else local
    return jax.shard_map(
        body,
        mesh=mesh,
        in_specs=placed,
        out_specs=(P("section", None, None), P("section", None, None), P("section", None, None)),
        check_vma=False,
    )
```
